128 devices in a mesh: dp: 32 (over y, x, core), rep: 4 (over z).
Axes of the slice: x: 4, y: 4, z: 4, core: 2. Of those that a mesh axis runs over, the one named last changes fastest.
Arguments:
- residual: float32 [2, 32, 1024, 768], P(None, 'dp', 'rep'), may hold values from -6 to 6
- lengths: int32 [2, 32], P(None, 'dp'), may hold values from 256 to 1024, as said below
- norm_gain: bfloat16 [768], P('dp'), may hold values from 0.5 to 1.5
- expand: bfloat16 [768, 3352], P('dp'), may hold values from -0.21875 to 0.21875
- filters: bfloat16 [1792, 4], P('dp'), may hold values from -3 to 3
- offsets: bfloat16 [1792], P('dp'), may hold values from -3 to 3
- gate_gain: bfloat16 [1536], P('dp'), may hold values from 0.5 to 1.5
- contract: bfloat16 [1536, 768], P('dp'), may hold values from -0.15625 to 0.15625
- step_bias: float32 [24], replicated, may hold values from -3 to 0.5
- decay_log: float32 [24], replicated, may hold values from -7 to -1.5
- skip_gain: float32 [24], replicated, may hold values from 0.5 to 1.5
- cotangent: float32 [2, 32, 1024, 768], P(None, 'dp', 'rep'), may hold values from -6 to 6
Outputs:
- mixed: float32 [2, 32, 1024, 768], P(None, 'dp', 'rep')
- residual_grad: float32 [2, 32, 1024, 768], P(None, 'dp', 'rep')
- norm_grad: float32 [768], P('dp')
- expand_grad: float32 [768, 3352], P('dp')
- filters_grad: float32 [1792, 4], P('dp')
- offsets_grad: float32 [1792], P('dp')
- gain_grad: float32 [1536], P('dp')
- contract_grad: float32 [1536, 768], P('dp')
- bias_grad: float32 [24], replicated
- decay_grad: float32 [24], replicated
- skip_grad: float32 [24], replicated
The draws below stay inside these ranges and needn't reach their ends.
Inputs may be any that keep to these rules, and one draw needn't show every extreme that they name: `lengths`: in each micro-batch one sequence has length 1024.
All inputs are finite; a program needn't handle non-finite values.
Results may differ from the reference program's by a relative error of at most 0.002.
The reference program's roundings to bfloat16 on the way count: a program that leaves them out, or rounds other values in their place, can miss the bound.
Values may be sent and summed in bfloat16 or wider, within the bound.
No kernel may reach another device: no remote copies, remote signals or barrier semaphores. Data moves between devices by JAX's collectives and lax.ppermute only.
A program may use at most 192 MiB of HBM per device.

```python
import jax
import jax.numpy as jnp
from jax import lax

D = 768
HEADS = 24
KERNEL = 4
BLOCK = 256
MICRO = 2
D_INNER = 1536
CONV_CH = 1792
PROJ = 3352
SEQLEN = 1024
SEQS = 32


def draw_lengths(key, part):
    key = jax.random.fold_in(key, 11)
    first, second = jax.random.split(key)
    drawn = jax.random.randint(first, (MICRO, SEQS), SEQLEN // 4, SEQLEN + 1)
    chosen = jax.random.randint(second, (MICRO, 1), 0, SEQS)
    slot = jnp.arange(SEQS)
    return jnp.where(slot[None, :] == chosen, SEQLEN, drawn).astype(jnp.int32)


def steps_of(own_key, extent, pieces, low, largest):
    loudness, own = 1.0, jax.random.fold_in(own_key, 6)
    for dim, shards_of in pieces:
        steps = jnp.exp(jax.random.uniform(jax.random.fold_in(own, dim), (shards_of,), jnp.float32, low / len(pieces), largest / len(pieces)))
        loudness = loudness * jnp.repeat(steps, extent[dim] // shards_of).reshape([-1 if axis == dim else 1 for axis in range(len(extent))])
    return loudness


def scatter_about(key, dims, width, bound, shards=(), dtype=jnp.bfloat16):
    array = width * jax.random.normal(key, dims, jnp.float32)
    if shards:
        array = array * steps_of(key, dims, shards, -0.22, 0.18)
    return jnp.clip(array, -bound, bound).astype(dtype)


def setup_inputs(seed: int = 0) -> dict:
    keys = jax.random.split(jax.random.key(seed), 13)
    residual = scatter_about(keys[0], (MICRO, SEQS, SEQLEN, D), 1.0, 6.0, ((1, 32), (2, 4)), jnp.float32)
    lengths = draw_lengths(jax.random.fold_in(keys[12], 71), 0)
    norm_gain = jnp.clip(1.0 + 0.1 * jax.random.normal(keys[2], (D,), jnp.float32), 0.5, 1.5).astype(jnp.bfloat16)
    expand = scatter_about(keys[3], (D, PROJ), D ** -0.5, 0.21875, ((0, 32),))
    filters = scatter_about(keys[4], (CONV_CH, KERNEL), KERNEL ** -0.5, 3.0, ((0, 32),))
    offsets = scatter_about(keys[5], (CONV_CH,), 0.5, 3.0, ((0, 32),))
    gate_gain = jnp.clip(1.0 + 0.1 * jax.random.normal(keys[6], (D_INNER,), jnp.float32), 0.5, 1.5).astype(jnp.bfloat16)
    contract = scatter_about(keys[7], (D_INNER, D), D_INNER ** -0.5, 0.15625, ((0, 32),))
    step_bias = jnp.clip(jax.random.uniform(keys[8], (HEADS,), jnp.float32, -3.0, 0.5), -3.0, 0.5)
    decay_log = jnp.clip(jax.random.uniform(keys[9], (HEADS,), jnp.float32, -7.0, -1.5), -7.0, -1.5)
    skip_gain = jnp.clip(jax.random.uniform(keys[10], (HEADS,), jnp.float32, 0.5, 1.5), 0.5, 1.5)
    cotangent = scatter_about(keys[11], (MICRO, SEQS, SEQLEN, D), 1.0, 6.0, ((1, 32), (2, 4)), jnp.float32)
    return {"residual": residual, "lengths": lengths, "norm_gain": norm_gain, "expand": expand, "filters": filters, "offsets": offsets, "gate_gain": gate_gain, "contract": contract, "step_bias": step_bias, "decay_log": decay_log, "skip_gain": skip_gain, "cotangent": cotangent}


@jax.custom_vjp
def low(v):
    return lax.optimization_barrier(v.astype(jnp.bfloat16)).astype(jnp.float32)

@jax.custom_vjp
def low_back(v):
    return v

def low_keep(v):
    return (low(v), None)

def low_pass(kept, grad):
    return (grad,)

def back_keep(v):
    return (v, None)

def back_low(kept, grad):
    return (low(grad),)
low.defvjp(low_keep, low_pass)
low_back.defvjp(back_keep, back_low)
epsilon = 1e-05
precise = lax.Precision.HIGHEST

def block_step(state, inputs):
    values, step, log_decay, writer, reader = inputs
    cumulative = jnp.cumsum(log_decay, axis=0)
    order = jnp.arange(log_decay.shape[0])
    causal = (order[:, None] >= order[None, :])[:, :, None]
    gaps = cumulative[:, None, :] - cumulative[None, :, :]
    decay = jnp.where(causal, jnp.exp(jnp.where(causal, gaps, 0.0)), 0.0)
    scores = jnp.dot(reader, writer.T, precision=precise)
    weights = scores[:, :, None] * decay * step[None, :, :]
    inner = jnp.einsum('tsh,shp->thp', weights, values, precision=precise)
    carried = jnp.einsum('tn,hpn->thp', reader, state, precision=precise) * jnp.exp(cumulative)[:, :, None]
    last = cumulative[-1]
    ends = jnp.exp(last[None, :] - cumulative) * step
    new_state = jnp.exp(last)[:, None, None] * state + jnp.einsum('sh,shp,sn->hpn', ends, values, writer, precision=precise)
    return (new_state, inner + carried)

def run_sequence(sequence, length, params):
    norm_gain, expand, filters, offsets, gate_gain, contract, step_bias, decay_log, skip_gain = params
    total = sequence.shape[0]
    inner_width = contract.shape[0]
    heads = step_bias.shape[0]
    head_size = inner_width // heads
    state_size = (expand.shape[1] - 2 * inner_width - heads) // 2
    kernel = filters.shape[1]
    mask = (jnp.arange(total) < length).astype(jnp.float32)[:, None]
    scale_one = lax.rsqrt(lax.optimization_barrier(jnp.mean(sequence * sequence, axis=-1, keepdims=True)) + epsilon)
    normed = low(sequence * scale_one * norm_gain)
    projected = low_back(jnp.dot(normed, expand, precision=precise))
    gate = projected[:, :inner_width]
    signal = projected[:, inner_width:2 * inner_width + 2 * state_size]
    step_raw = projected[:, 2 * inner_width + 2 * state_size:]
    padded = jnp.concatenate([jnp.zeros((kernel - 1, signal.shape[1]), jnp.float32), signal], axis=0)
    filtered = offsets
    for tap in range(kernel):
        filtered = filtered + filters[:, tap] * padded[tap:tap + total]
    activated = jax.nn.silu(filtered)
    values = activated[:, :inner_width].reshape(total, heads, head_size)
    writer = activated[:, inner_width:inner_width + state_size]
    reader = activated[:, inner_width + state_size:]
    step = jax.nn.softplus(step_raw + step_bias)
    log_decay = -step * jnp.exp(decay_log)
    blocks = total // BLOCK
    initial = jnp.zeros((heads, head_size, state_size), jnp.float32)
    _, outputs = lax.scan(jax.checkpoint(block_step), initial, (values.reshape(blocks, BLOCK, heads, head_size), step.reshape(blocks, BLOCK, heads), log_decay.reshape(blocks, BLOCK, heads), writer.reshape(blocks, BLOCK, state_size), reader.reshape(blocks, BLOCK, state_size)))
    outputs = outputs.reshape(total, heads, head_size) + skip_gain[:, None] * values
    gated = outputs.reshape(total, inner_width) * jax.nn.silu(gate)
    scale_two = lax.rsqrt(lax.optimization_barrier(jnp.mean(gated * gated, axis=-1, keepdims=True)) + epsilon)
    normed_out = low(gated * scale_two * gate_gain)
    branch = low_back(jnp.dot(normed_out, contract, precision=precise))
    return sequence + mask * branch

def reference(residual, lengths, norm_gain, expand, filters, offsets, gate_gain, contract, step_bias, decay_log, skip_gain, cotangent):
    params = tuple((item.astype(jnp.float32) for item in (norm_gain, expand, filters, offsets, gate_gain, contract, step_bias, decay_log, skip_gain)))
    flat = residual.reshape(-1, residual.shape[2], residual.shape[3])
    flat_lengths = lengths.reshape(-1)

    def forward(flat_in, params_in):

        def single(pair):
            return run_sequence(pair[0], pair[1], params_in)
        return lax.map(jax.checkpoint(single), (flat_in, flat_lengths))
    mixed, pull = jax.vjp(forward, flat, params)
    flat_grad, grads = pull(cotangent.reshape(flat.shape))
    norm_grad, expand_grad, filters_grad, offsets_grad, gain_grad, contract_grad, bias_grad, decay_grad, skip_grad = grads
    return (mixed.reshape(residual.shape), flat_grad.reshape(residual.shape), norm_grad, expand_grad, filters_grad, offsets_grad, gain_grad, contract_grad, bias_grad, decay_grad, skip_grad)
```

```python
import functools

import jax
import jax.numpy as jnp
import numpy as np
from jax import lax
from jax.experimental import pallas as pl
from jax.experimental.pallas import tpu as pltpu
from jax.sharding import Mesh
from jax.sharding import PartitionSpec as P

EPS = 1e-05
DP = ("y", "x", "core")
F32 = jnp.float32
BF16 = jnp.bfloat16
HIGHEST = lax.Precision.HIGHEST
NN = (((1,), (0,)), ((), ()))
NT = (((1,), (1,)), ((), ()))
TN = (((0,), (0,)), ((), ()))
VMEM_LIMIT = 56 * 1024 * 1024


def shifted(x, axis, shift):
    n = lax.axis_size(axis)
    return lax.ppermute(x, axis, [(i, (i + shift) % n) for i in range(n)])


def in_order(rel, axis):
    n = lax.axis_size(axis)
    i = lax.axis_index(axis)
    twice = jnp.stack(rel + rel)
    return lax.dynamic_slice_in_dim(twice, (n - i) % n, n, 0)


def halves(x):
    h = x.shape[0] // 2
    return x[:h], x[h:]


def gather(x, axis, ring=False):
    n = lax.axis_size(axis)
    if n == 1:
        return x[None]
    if n == 4 and ring:
        left = shifted(x, axis, 1)
        right = shifted(x, axis, -1)
        far = jnp.concatenate(
            [shifted(halves(left)[0], axis, 1), shifted(halves(right)[1], axis, -1)], axis=0
        )
        return in_order([x, right, far, left], axis)
    return in_order([x] + [shifted(x, axis, -k) for k in range(1, n)], axis)


def block_at(x, index, dim):
    return lax.dynamic_index_in_dim(x, index, dim, keepdims=False)


def scatter_sum(x, axis, dim=0):
    n = lax.axis_size(axis)
    if n == 1:
        return block_at(x, 0, dim)
    i = lax.axis_index(axis)
    total = block_at(x, i, dim)
    for k in range(1, n):
        total = total + shifted(block_at(x, (i + k) % n, dim), axis, k)
    return total


def exchange(x, axis):
    n = lax.axis_size(axis)
    i = lax.axis_index(axis)
    rel = [block_at(x, i, 0)]
    for k in range(1, n):
        rel.append(shifted(block_at(x, (i - k) % n, 0), axis, -k))
    return in_order(rel, axis)


def sum_over(x, axis):
    total = x
    for k in range(1, lax.axis_size(axis)):
        total = total + shifted(x, axis, k)
    return total


def gather_dp(x):
    shape = x.shape
    for axis in ("x", "y", "core"):
        x = gather(x, axis)
    x = jnp.transpose(x, (1, 2, 0) + tuple(range(3, x.ndim)))
    return x.reshape((-1,) + shape)


def scatter_dp(x, shape):
    y, xs, core = (lax.axis_size(a) for a in DP)
    x = x.reshape((y, xs, core) + shape)
    x = scatter_sum(x, "core", 2)
    x = scatter_sum(x, "x", 1)
    return scatter_sum(x, "y", 0)


def dot(a, b, dims=NN):
    return lax.dot_general(a, b, dims, preferred_element_type=F32)


def exact(a, b, dims=NN):
    return lax.dot_general(a, b, dims, precision=HIGHEST, preferred_element_type=F32)


def split(a):
    hi = a.astype(BF16)
    return hi, (a - hi.astype(F32)).astype(BF16)


def dot3(a, b, dims=NN):
    ah, al = split(a)
    bh, bl = split(b)
    return dot(ah, bh, dims) + (dot(ah, bl, dims) + dot(al, bh, dims))


def sigmoid(v):
    return 1.0 / (1.0 + jnp.exp(-v))


def steps_of(sr, hp, heads):
    lane = lax.broadcasted_iota(jnp.int32, sr.shape, 1)
    shifted_raw = sr + hp[0:1]
    step = jnp.maximum(shifted_raw, 0.0) + jnp.log1p(jnp.exp(-jnp.abs(shifted_raw)))
    step = jnp.where(lane < heads, step, 0.0)
    return shifted_raw, step, -step * hp[1:2]


def triangle(q, lower):
    row = lax.broadcasted_iota(jnp.int32, (q, q), 0)
    col = lax.broadcasted_iota(jnp.int32, (q, q), 1)
    return (row >= col) if lower else (col >= row)


def forward_kernel(
    heads, nb, bg, w, co, fp, hp, cp, oh,
    gate_o, sig_o, pre_o, y_o, oc_o, sr_o, sin_o, sums_o,
    state, tail,
):
    q = nb.shape[0]
    ch = cp.shape[1]
    cw = fp.shape[1]
    ns = (cw - ch) // 2
    size = ch // heads

    @pl.when(pl.program_id(0) == 0)
    def _():
        state[...] = jnp.zeros_like(state)
        tail[...] = jnp.zeros_like(tail)

    proj = dot(nb[...], w[...])
    gate = proj[:, :ch]
    signal = proj[:, ch : ch + cw]
    lane = lax.broadcasted_iota(jnp.int32, (q, 128), 1)
    sr = jnp.where(lane < heads, proj[:, ch + cw : ch + cw + 128], 0.0)
    ext = jnp.concatenate([tail[...], signal], axis=0)
    pre = fp[4:5, :] + jnp.zeros_like(signal)
    for k in range(4):
        pre = pre + fp[k : k + 1, :] * ext[5 + k : 5 + k + q]
    tail[...] = signal[q - 8 :]
    act = pre * sigmoid(pre)
    values = act[:, :ch]
    writer = act[:, ch : ch + ns]
    reader = act[:, ch + ns :]
    _, step, ld = steps_of(sr, hp[...], heads)
    lower = triangle(q, True)
    cum = exact(jnp.where(lower, 1.0, 0.0), ld)
    cum_t = cum.T
    cum_e = exact(cum, oh[...])
    step_e = exact(step, oh[...])
    last_e = cum_e[q - 1 : q]
    xv = step_e * values
    scores = dot3(reader, writer, NT)
    parts = []
    for p in range(ch // 128):
        hi, lo = split(xv[:, 128 * p : 128 * p + 128])
        both = jnp.concatenate([hi, lo], axis=1)
        out = None
        for j in range(128 // size):
            h = p * (128 // size) + j
            decay = jnp.exp(cum[:, h : h + 1] - cum_t[h : h + 1, :])
            ph, plo = split(jnp.where(lower, scores * decay, 0.0))
            r = dot(ph, both)
            one = r[:, :128] + (r[:, 128:] + dot(plo, hi))
            out = one if out is None else jnp.where(lane < j * size, out, one)
        parts.append(out)
    inner = jnp.concatenate(parts, axis=1)
    old = state[...]
    sin_o[0] = old
    y = inner + jnp.exp(cum_e) * dot3(reader, old, NT) + cp[0:1, :] * values
    decay_last = jnp.exp(cum_t[:, q - 1 : q])
    decay_ch = exact(oh[...], decay_last * jnp.ones((1, ns), F32), TN)
    state[...] = decay_ch * old + dot3(jnp.exp(last_e - cum_e) * xv, writer, TN)
    gated = y * (gate * sigmoid(gate))
    outcome = dot(bg[...], co[...], NT)
    ones = jnp.ones((8, ch), F32)
    s1 = exact(ones, gated * gated, NT)
    s2 = exact(ones, outcome * cp[1:2, :] * gated, NT)
    row = lax.broadcasted_iota(jnp.int32, s1.shape, 0)
    sums_o[...] = jnp.where(row == 0, s1, jnp.where(row == 1, s2, 0.0))
    gate_o[...] = gate
    sig_o[...] = signal
    pre_o[...] = pre
    y_o[...] = y
    oc_o[...] = outcome
    sr_o[...] = sr


def gate_kernel(width, gate_r, y_r, oc_r, sums, bg, cp, nout_o, gg_o, dy_o, cg_o, acc_o):
    q, ch = gate_r.shape

    @pl.when(pl.program_id(0) == 0)
    def _():
        cg_o[...] = jnp.zeros_like(cg_o)
        acc_o[...] = jnp.zeros_like(acc_o)

    s = sums[...]
    scale_row = lax.rsqrt(s[0:1] * (1.0 / width) + EPS)
    mean_row = scale_row * s[1:2] * (1.0 / width)

    def column(v):
        c = jnp.broadcast_to(v, (128, q)).T
        return jnp.concatenate([c] * (ch // 128), axis=1)

    scale = column(scale_row)
    mean = column(mean_row)
    gate = gate_r[...]
    y = y_r[...]
    outcome = oc_r[...]
    gain = cp[1:2, :]
    sg = sigmoid(gate)
    sl = gate * sg
    unit = y * sl * scale
    nout = (unit * gain).astype(BF16)
    nout_o[...] = nout
    cg_o[...] += dot(nout, bg[...], TN)
    gated_grad = scale * (outcome * gain - unit * mean)
    dy_o[...] = gated_grad * sl
    gg_o[...] = (gated_grad * y * sg * (1.0 + gate * (1.0 - sg))).astype(BF16)
    gain_part = jnp.sum(outcome * unit, axis=0, keepdims=True)
    row = lax.broadcasted_iota(jnp.int32, acc_o.shape, 0)
    acc_o[...] += jnp.where(row == 0, gain_part, 0.0)


def backward_kernel(
    heads, sig_r, pre_r, y_r, dy_r, sr_r, sin_r, fp, hp, cp, oh,
    vg_o, wr_o, raw_o, acc_o, hacc_o,
    adj, head_rows,
):
    q, ch = y_r.shape
    cw = fp.shape[1]
    ns = (cw - ch) // 2
    size = ch // heads

    @pl.when(pl.program_id(0) == 0)
    def _():
        adj[...] = jnp.zeros_like(adj)
        head_rows[...] = jnp.zeros_like(head_rows)
        acc_o[...] = jnp.zeros_like(acc_o)
        hacc_o[...] = jnp.zeros_like(hacc_o)

    pre = pre_r[...]
    sgm = sigmoid(pre)
    act = pre * sgm
    values = act[:, :ch]
    writer = act[:, ch : ch + ns]
    reader = act[:, ch + ns :]
    shifted_raw, step, ld = steps_of(sr_r[...], hp[...], heads)
    lower = triangle(q, True)
    upper = triangle(q, False)
    cum = exact(jnp.where(lower, 1.0, 0.0), ld)
    cum_t = cum.T
    cum_e = exact(cum, oh[...])
    step_e = exact(step, oh[...])
    last_e = cum_e[q - 1 : q]
    skip = cp[0:1, :]
    dy = dy_r[...]
    y = y_r[...]
    xv = step_e * values
    lane = lax.broadcasted_iota(jnp.int32, (q, 128), 1)
    scores = dot3(writer, reader, NT)
    dscores = jnp.zeros((q, q), F32)
    parts = []
    for p in range(ch // 128):
        dpair = dy[:, 128 * p : 128 * p + 128]
        xpair = xv[:, 128 * p : 128 * p + 128]
        dh, dl = split(dpair)
        dboth = jnp.concatenate([dh, dl], axis=1)
        dtwice = jnp.concatenate([dh, dh], axis=1)
        out = None
        for j in range(128 // size):
            h = p * (128 // size) + j
            decay = jnp.where(upper, jnp.exp(cum_t[h : h + 1, :] - cum[:, h : h + 1]), 0.0)
            ph, plo = split(jnp.where(upper, scores * decay, 0.0))
            r = dot(ph, dboth)
            one = r[:, :128] + (r[:, 128:] + dot(plo, dh))
            out = one if out is None else jnp.where(lane < j * size, out, one)
            mine = (lane >= j * size) & (lane < (j + 1) * size)
            xh, xl = split(jnp.where(mine, xpair, 0.0))
            m = dot(jnp.concatenate([xh, xl], axis=1), dtwice, NT) + dot(xh, dl, NT)
            dscores = dscores + m * decay
        parts.append(out)
    inner = jnp.concatenate(parts, axis=1)
    old = adj[...]
    sin = sin_r[0]
    ends = jnp.exp(last_e - cum_e)
    from_state = ends * dot3(writer, old, NT)
    dxv = inner + from_state
    cdy = jnp.exp(cum_e) * dy
    dwriter = dot3(dscores, reader) + dot3(ends * xv, old)
    dreader = dot3(dscores, writer, TN) + dot3(cdy, sin)
    decay_last = jnp.exp(cum_t[:, q - 1 : q])
    decay_ch = exact(oh[...], decay_last * jnp.ones((1, ns), F32), TN)
    state_part = decay_ch * old * sin
    ones = jnp.ones((8, ns), F32)
    state_row = exact(ones, state_part, NT)[0:1]
    last_row = state_row + jnp.sum(xv * from_state, axis=0, keepdims=True)
    adj[...] = decay_ch * old + dot3(cdy, reader, TN)

    dstep = exact(values * dxv, oh[...], NT)
    row = lax.broadcasted_iota(jnp.int32, (q, ch), 0)
    dcum_ch = dy * (y - skip * values) - xv * dxv + jnp.where(row == q - 1, last_row, 0.0)
    dcum = exact(dcum_ch, oh[...], NT)
    dld = exact(jnp.where(upper, 1.0, 0.0), dcum)
    raw = (dstep - dld * hp[1:2]) * sigmoid(shifted_raw)
    raw = jnp.where(lane < heads, raw, 0.0)
    raw_o[...] = raw.astype(BF16)
    hrow = lax.broadcasted_iota(jnp.int32, hacc_o.shape, 0)
    hacc_o[...] += jnp.where(
        hrow == 0,
        jnp.sum(raw, axis=0, keepdims=True),
        jnp.where(hrow == 1, jnp.sum(dld * ld, axis=0, keepdims=True), 0.0),
    )

    wr_o[...] = jnp.concatenate([dwriter, dreader], axis=1)
    sv = sgm[:, :ch]
    dpre = (step_e * dxv + skip * dy) * (sv * (1.0 + pre[:, :ch] * (1.0 - sv)))
    ext = jnp.concatenate([dpre, head_rows[...]], axis=0)
    head_rows[...] = dpre[:8]
    signal = sig_r[:, :ch]
    total = jnp.zeros_like(dpre)
    rows = []
    for k in range(4):
        moved = ext[3 - k : 3 - k + q]
        total = total + fp[k : k + 1, :ch] * moved
        rows.append(jnp.sum(moved * signal, axis=0, keepdims=True))
    vg_o[...] = total.astype(BF16)
    rows.append(jnp.sum(dpre, axis=0, keepdims=True))
    rows.append(jnp.sum(values * dy, axis=0, keepdims=True))
    rows.append(jnp.zeros((2, ch), F32))
    acc_o[...] += jnp.concatenate(rows, axis=0)


def whole(shape):
    return pl.BlockSpec(shape, lambda b: (0,) * len(shape))


def rows_of(q, width, order=lambda b: b):
    return pl.BlockSpec((q, width), lambda b: (order(b), 0))


def params(flops, nbytes):
    return dict(
        compiler_params=pltpu.CompilerParams(
            dimension_semantics=("arbitrary",), vmem_limit_bytes=VMEM_LIMIT
        ),
        cost_estimate=pl.CostEstimate(flops=flops, bytes_accessed=nbytes, transcendentals=0),
    )


def body(
    residual, lengths, norm_gain, expand, filters, offsets, gate_gain, contract,
    step_bias, decay_log, skip_gain, cotangent,
):
    micro, _, q, width = residual.shape
    heads_all = step_bias.shape[0]
    reps = lax.axis_size("rep")
    heads = heads_all // reps
    dp = lax.axis_size("y") * lax.axis_size("x") * lax.axis_size("core")
    inner = contract.shape[0] * dp
    ch = inner // reps
    conv = filters.shape[0] * dp
    ns = (conv - inner) // 2
    cw = ch + 2 * ns
    size = inner // heads_all
    total = q * reps
    rep = lax.axis_index("rep")
    rows = expand.shape[0]
    wr = 2 * ns // reps
    residual = residual[:, 0]
    cotangent = cotangent[:, 0]

    small = jnp.concatenate([norm_gain, filters.reshape(-1), offsets, gate_gain])
    sizes = np.cumsum([0, norm_gain.shape[0], filters.size, offsets.shape[0], gate_gain.shape[0]])
    padded = -(-small.shape[0] // 128) * 128
    small = jnp.pad(small, (0, padded - small.shape[0])).reshape(-1, 128)
    position = rep * q + jnp.arange(q, dtype=jnp.int32)
    mask = (position[None, :] < lengths[:, :1]).astype(F32)[..., None]
    branch_grad = (mask * cotangent).astype(BF16)
    with jax.named_scope("gather_small"):
        small = gather_dp(small).reshape(dp, padded).astype(F32)
    gain_one = small[:, sizes[0] : sizes[1]].reshape(-1)
    filters_full = small[:, sizes[1] : sizes[2]].reshape(conv, 4).T
    offsets_full = small[:, sizes[2] : sizes[3]].reshape(1, conv)
    gain_two = small[:, sizes[3] : sizes[4]].reshape(1, inner)

    def own(a, start, count, dim=-1):
        return lax.dynamic_slice_in_dim(a, start + rep * count, count, a.ndim + dim)

    w_shard = jnp.concatenate(
        [
            own(expand, 0, ch),
            own(expand, inner, ch),
            expand[:, 2 * inner : 2 * inner + 2 * ns],
            jnp.pad(own(expand, 2 * inner + 2 * ns, heads), ((0, 0), (0, 128 - heads))),
        ],
        axis=1,
    )
    with jax.named_scope("gather_own_expand"):
        w_own = gather_dp(w_shard).reshape(width, ch + cw + 128)
    with jax.named_scope("gather_contract"):
        contract_full = lax.all_gather(contract, DP, axis=0, tiled=True)
    contract_own = lax.dynamic_slice_in_dim(contract_full, rep * ch, ch, 0)
    expand_cols = jnp.concatenate(
        [
            expand[:, :inner].reshape(rows, reps, ch),
            expand[:, inner : 2 * inner].reshape(rows, reps, ch),
            expand[:, 2 * inner : 2 * inner + 2 * ns].reshape(rows, reps, wr),
            expand[:, 2 * inner + 2 * ns :].reshape(rows, reps, heads),
            jnp.zeros((rows, reps, 128 - wr - heads), BF16),
        ],
        axis=2,
    ).reshape(rows, reps * (2 * ch + 128))
    with jax.named_scope("gather_expand"):
        expand_full = lax.all_gather(expand_cols, DP, axis=0, tiled=True)

    own_filters = jnp.concatenate(
        [own(filters_full[:, :inner], 0, ch), filters_full[:, inner:]], axis=1
    )
    own_offsets = jnp.concatenate(
        [own(offsets_full[:, :inner], 0, ch), offsets_full[:, inner:]], axis=1
    )
    fp = jnp.concatenate([own_filters, own_offsets, jnp.zeros((3, cw), F32)], axis=0)
    own_skip = own(skip_gain, 0, heads)
    cp = jnp.concatenate(
        [jnp.repeat(own_skip, size)[None], own(gain_two, 0, ch), jnp.zeros((6, ch), F32)], axis=0
    )
    rate = jnp.exp(own(decay_log, 0, heads))
    hp = jnp.pad(jnp.stack([own(step_bias, 0, heads), rate]), ((0, 6), (0, 128 - heads)))
    onehot = np.zeros((128, ch), np.float32)
    onehot[np.arange(ch) // size, np.arange(ch)] = 1.0
    onehot = jnp.asarray(onehot)

    scale_one = lax.rsqrt(jnp.mean(residual * residual, axis=-1, keepdims=True) + EPS)
    unit_one = residual * scale_one
    normed = (unit_one * gain_one).astype(BF16)

    full_bg, full_normed = [], []
    for m in range(micro):
        with jax.named_scope("gather_branch_grad"):
            full_bg.append(gather(branch_grad[m], "rep", ring=True).reshape(total, width))
        with jax.named_scope("gather_normed"):
            full_normed.append(gather(normed[m], "rep", ring=True).reshape(total, width))

    sds = jax.ShapeDtypeStruct
    forward = pl.pallas_call(
        functools.partial(forward_kernel, heads),
        grid=(reps,),
        in_specs=[
            rows_of(q, width), rows_of(q, width), whole((width, ch + cw + 128)), whole((ch, width)),
            whole((8, cw)), whole((8, 128)), whole((8, ch)), whole((128, ch)),
        ],
        out_specs=[
            rows_of(q, ch), rows_of(q, cw), rows_of(q, cw), rows_of(q, ch), rows_of(q, ch),
            rows_of(q, 128), pl.BlockSpec((1, ch, ns), lambda b: (b, 0, 0)),
            pl.BlockSpec((8, q), lambda b: (0, b)),
        ],
        out_shape=[
            sds((total, ch), F32), sds((total, cw), F32), sds((total, cw), F32),
            sds((total, ch), F32), sds((total, ch), F32), sds((total, 128), F32),
            sds((reps, ch, ns), F32), sds((8, total), F32),
        ],
        scratch_shapes=[pltpu.VMEM((ch, ns), F32), pltpu.VMEM((8, cw), F32)],
        name="scan_forward",
        **params(20_000_000_000, 20_000_000),
    )
    gating = pl.pallas_call(
        functools.partial(gate_kernel, inner),
        grid=(reps,),
        in_specs=[
            rows_of(q, ch), rows_of(q, ch), rows_of(q, ch),
            pl.BlockSpec((8, q), lambda b: (0, b)), rows_of(q, width), whole((8, ch)),
        ],
        out_specs=[
            rows_of(q, ch), rows_of(q, ch), rows_of(q, ch), whole((ch, width)), whole((8, ch)),
        ],
        out_shape=[
            sds((total, ch), BF16), sds((total, ch), BF16), sds((total, ch), F32),
            sds((ch, width), F32), sds((8, ch), F32),
        ],
        name="gate_backward",
        **params(4_000_000_000, 10_000_000),
    )
    back = lambda b: reps - 1 - b
    backward = pl.pallas_call(
        functools.partial(backward_kernel, heads),
        grid=(reps,),
        in_specs=[
            rows_of(q, cw, back), rows_of(q, cw, back), rows_of(q, ch, back), rows_of(q, ch, back),
            rows_of(q, 128, back), pl.BlockSpec((1, ch, ns), lambda b: (back(b), 0, 0)),
            whole((8, cw)), whole((8, 128)), whole((8, ch)), whole((128, ch)),
        ],
        out_specs=[
            rows_of(q, ch, back), rows_of(q, 2 * ns, back), rows_of(q, 128, back),
            whole((8, ch)), whole((8, 128)),
        ],
        out_shape=[
            sds((total, ch), BF16), sds((total, 2 * ns), F32), sds((total, 128), BF16),
            sds((8, ch), F32), sds((8, 128), F32),
        ],
        scratch_shapes=[pltpu.VMEM((ch, ns), F32), pltpu.VMEM((8, ch), F32)],
        name="scan_backward",
        **params(40_000_000_000, 20_000_000),
    )

    wr_filters = own(filters_full[:, inner:], 0, wr)
    sums = []
    kept = []
    for m in range(micro):
        out = forward(full_normed[m], full_bg[m], w_own, contract_own, fp, hp, cp, onehot)
        kept.append(out)
        with jax.named_scope("sum_norm_terms"):
            sums.append(sum_over(out[7], "rep"))
    mixed, gate_grads, dys, back_nout = [], [], [], []
    contract_part = 0.0
    gain_part = 0.0
    for m in range(micro):
        gate, _, _, y, outcome, _, _, _ = kept[m]
        nout, gg, dy, cg, acc = gating(gate, y, outcome, sums[m], full_bg[m], cp)
        gate_grads.append(gg)
        dys.append(dy)
        contract_part = contract_part + cg
        gain_part = gain_part + acc[0]
        back_nout.append(nout)
    own_pg = []
    for m in range(micro):
        with jax.named_scope("send_gate_parts"):
            both = jnp.concatenate([back_nout[m], gate_grads[m]], axis=1).reshape(reps, q, 2 * ch)
            got = exchange(both, "rep")
        nout_own = jnp.concatenate([got[s, :, :ch] for s in range(reps)], axis=1)
        branch = jnp.dot(nout_own, contract_full, preferred_element_type=F32)
        mixed.append(residual[m] + mask[m] * branch)
        own_pg.append(got[:, :, ch:])
    with jax.named_scope("sum_contract_grad"):
        cgs = contract_part.reshape(lax.axis_size("x"), lax.axis_size("core"), -1, width)
        cgs = scatter_sum(cgs, "core", 1)
        cgs = scatter_sum(cgs, "x", 0)
        ys = lax.axis_size("y")
        cgs = cgs.reshape(ys, -1, width)
        cgs = scatter_sum(cgs, "y", 0)
        cgs = lax.ppermute(
            cgs, ("y", "rep"), [(a * reps + b, b * reps + a) for a in range(ys) for b in range(reps)]
        )
        contract_grad = gather(cgs, "rep").reshape(-1, width)

    normed_all = jnp.concatenate(full_normed, axis=0)
    with jax.named_scope("sum_expand_grad_gate"):
        gate_all = jnp.concatenate(gate_grads, axis=0)
        eg_gate = lax.dot_general(normed_all, gate_all, TN, preferred_element_type=F32)
        eg_gate = scatter_dp(eg_gate, (rows, ch))

    value_grads, tails, channel_part, head_part, wr_part = [], [], 0.0, 0.0, 0.0
    grads = []
    for m in range(micro):
        _, signal, pre, y, _, sr, sin, _ = kept[m]
        vg, wrg, raw, acc, hacc = backward(signal, pre, y, dys[m], sr, sin, fp, hp, cp, onehot)
        value_grads.append(vg)
        channel_part = channel_part + acc
        head_part = head_part + hacc
        with jax.named_scope("sum_writer_reader_grad"):
            t = wrg.reshape(2, total // 2, reps, wr)
            t = jnp.transpose(t, (2, 1, 0, 3)).reshape(reps, total // 2, 2 * wr)
            t = scatter_sum(t, "rep", 0)
            t = jnp.transpose(t.reshape(total // 2, 2, wr), (1, 0, 2)).reshape(total, wr)
        pre_wr = own(pre[:, ch:], 0, wr)
        sig_wr = own(signal[:, ch:], 0, wr)
        s = jax.nn.sigmoid(pre_wr)
        dpre = t * (s * (1.0 + pre_wr * (1.0 - s)))
        ext = jnp.pad(dpre, ((0, 3), (0, 0)))
        wr_grad = jnp.zeros_like(dpre)
        parts = []
        for k in range(4):
            moved = ext[3 - k : 3 - k + total]
            wr_grad = wr_grad + wr_filters[k][None] * moved
            parts.append(jnp.sum(moved * sig_wr, axis=0))
        parts.append(jnp.sum(dpre, axis=0))
        wr_part = wr_part + jnp.stack(parts)
        tails.append(
            jnp.concatenate(
                [wr_grad.astype(BF16), raw[:, :heads], jnp.zeros((total, 128 - wr - heads), BF16)],
                axis=1,
            )
        )
    for m in range(micro):
        with jax.named_scope("send_value_grad"):
            vgs = exchange(value_grads[m].reshape(reps, q, ch), "rep")
        with jax.named_scope("send_tail_grad"):
            tls = exchange(tails[m].reshape(reps, q, 128), "rep")
        pg = jnp.concatenate([own_pg[m], vgs, tls], axis=2)
        pg = jnp.concatenate([pg[s] for s in range(reps)], axis=1)
        grads.append(lax.dot_general(pg, expand_full, NT, preferred_element_type=F32))
    with jax.named_scope("sum_expand_grad_values"):
        vg_all = jnp.concatenate(value_grads, axis=0)
        eg_values = lax.dot_general(normed_all, vg_all, TN, preferred_element_type=F32)
        eg_values = scatter_dp(eg_values, (rows, ch))
    with jax.named_scope("sum_expand_grad_tail"):
        tail_all = jnp.concatenate(tails, axis=0)
        eg_tail = lax.dot_general(normed_all, tail_all, TN, preferred_element_type=F32)
        eg_tail = scatter_dp(eg_tail, (rows, 128))
    with jax.named_scope("gather_expand_grad"):
        eg = gather(jnp.concatenate([eg_gate, eg_values, eg_tail], axis=1), "rep")
    expand_grad = jnp.concatenate(
        [eg[s, :, a:b] for a, b in ((0, ch), (ch, 2 * ch), (2 * ch, 2 * ch + wr), (2 * ch + wr, 2 * ch + wr + heads)) for s in range(reps)],
        axis=1,
    )

    normed_grad = jnp.stack(grads)
    norm_part = jnp.sum(normed_grad * unit_one, axis=(0, 1))
    scaled = normed_grad * gain_one
    residual_grad = cotangent + scale_one * (
        scaled - unit_one * jnp.mean(scaled * unit_one, axis=-1, keepdims=True)
    )

    def sum_dp(v):
        n = v.shape[0]
        v = jnp.pad(v, (0, -n % 1024)).reshape(-1, 128)
        for axis in ("core", "x", "y"):
            v = sum_over(v, axis)
        return v

    with jax.named_scope("sum_small"):
        flat = jnp.concatenate(
            [channel_part[:6].reshape(-1), gain_part, head_part[:2].reshape(-1), wr_part.reshape(-1)]
        )
        flat = gather(sum_dp(flat), "rep").reshape(reps, -1)
    cuts = np.cumsum([0, 6 * ch, ch, 256, 5 * wr])
    channels = flat[:, : cuts[1]].reshape(reps, 6, ch)
    gain_all = flat[:, cuts[1] : cuts[2]].reshape(-1)
    head_all = flat[:, cuts[2] : cuts[3]].reshape(reps, 2, 128)[:, :, :heads]
    wr_all = flat[:, cuts[3] : cuts[4]].reshape(reps, 5, wr)
    taps = jnp.concatenate(
        [
            jnp.transpose(channels[:, :5], (1, 0, 2)).reshape(5, inner),
            jnp.transpose(wr_all, (1, 0, 2)).reshape(5, 2 * ns),
        ],
        axis=1,
    )
    place = lax.axis_index(DP)
    mine = lambda a: lax.dynamic_slice_in_dim(a, place * (a.shape[-1] // dp), a.shape[-1] // dp, a.ndim - 1)
    own_taps = mine(taps)
    filters_grad = own_taps[:4].T
    offsets_grad = own_taps[4]
    gain_grad = mine(gain_all)
    skip_grad = jnp.sum(channels[:, 5].reshape(heads_all, size), axis=1)
    bias_grad = head_all[:, 0].reshape(-1)
    decay_grad = head_all[:, 1].reshape(-1)
    with jax.named_scope("sum_norm_grad"):
        norm_grad = mine(sum_over(sum_dp(norm_part), "rep").reshape(-1)[:width])

    return (
        jnp.stack(mixed)[:, None],
        residual_grad[:, None],
        norm_grad,
        expand_grad,
        filters_grad,
        offsets_grad,
        gain_grad,
        contract_grad,
        bias_grad,
        decay_grad,
        skip_grad,
    )


def solution(mesh):
    dp, rep = mesh.devices.shape
    core = 2 if dp % 8 == 0 else 1
    fine = Mesh(mesh.devices.reshape(rep, dp // (core * rep), core, rep), DP + ("rep",))
    rows = P(None, DP, "rep", None)
    in_specs = (
        rows, P(None, DP), P(DP), P(DP, None), P(DP, None), P(DP), P(DP), P(DP, None),
        P(), P(), P(), rows,
    )
    out_specs = (
        rows, rows, P(DP), P(DP, None), P(DP, None), P(DP), P(DP), P(DP, None), P(), P(), P(),
    )
    return jax.shard_map(body, mesh=fine, in_specs=in_specs, out_specs=out_specs, check_vma=False)
```

```python
import functools

import jax
import jax.numpy as jnp
import numpy as np
from jax import lax
from jax.experimental import pallas as pl
from jax.experimental.pallas import tpu as pltpu
from jax.sharding import PartitionSpec as P

EPS = 1e-05
F32 = jnp.float32
BF16 = jnp.bfloat16
NN = (((1,), (0,)), ((), ()))
NT = (((1,), (1,)), ((), ()))
TN = (((0,), (0,)), ((), ()))
VMEM_LIMIT = 56 * 1024 * 1024


class Axes:
    def __init__(self, dims):
        self.size = dict(zip(("y", "x", "core"), dims))
        place = lax.axis_index("dp")
        y, x, core = dims
        self.place = {
            "y": place // (x * core),
            "x": (place // core) % x,
            "core": place % core,
            "rep": lax.axis_index("rep"),
        }
        self.size["rep"] = lax.axis_size("rep")

    def shift(self, v, axis, by):
        n = self.size[axis]
        if axis == "rep":
            return lax.ppermute(v, "rep", [(i, (i + by) % n) for i in range(n)])
        stride = {"core": 1, "x": self.size["core"], "y": self.size["core"] * self.size["x"]}[axis]
        route = []
        for i in range(lax.axis_size("dp")):
            at = (i // stride) % n
            route.append((i, i + ((at + by) % n - at) * stride))
        return lax.ppermute(v, "dp", route)

    def near_ring(self, v):
        return self.shift(v, "rep", 1), self.shift(v, "rep", -1)

    def far_ring(self, v, left, right):
        far = (self.shift(left[:1], "rep", 1), self.shift(right[1:], "rep", -1))
        return [v, right, left, far[0], far[1]]

    def exchange(self, v, axis="rep"):
        n = self.size[axis]
        if n == 1:
            return v
        if axis == "rep":
            return lax.all_to_all(v, "rep", 0, 0, tiled=True)
        stride = {"core": 1, "x": self.size["core"], "y": self.size["core"] * self.size["x"]}[axis]
        starts = [i for i in range(lax.axis_size("dp")) if (i // stride) % n == 0]
        groups = [[i + k * stride for k in range(n)] for i in starts]
        return lax.all_to_all(v, "dp", 0, 0, axis_index_groups=groups, tiled=True)

    def everywhere(self, v, axis="rep"):
        return self.exchange(jnp.broadcast_to(v[None], (self.size[axis],) + v.shape), axis)

    def block(self, v, axis, ahead, dim):
        index = (self.place[axis] + ahead) % self.size[axis]
        return lax.dynamic_index_in_dim(v, index, dim, keepdims=False)

    def scatter_sum(self, v, axis, dim):
        total = self.block(v, axis, 0, dim)
        for k in range(1, self.size[axis]):
            total = total + self.shift(self.block(v, axis, k, dim), axis, k)
        return total


def dot(a, b, dims=NN):
    return lax.dot_general(a, b, dims, preferred_element_type=F32)


def split(a):
    hi = a.astype(BF16)
    return hi, (a - hi.astype(F32)).astype(BF16)


def dot3(a, b, dims=NN):
    ah, al = split(a)
    bh, bl = split(b)
    return dot(ah, bh, dims) + (dot(ah, bl, dims) + dot(al, bh, dims))


def dot2(a, b, dims=NN):
    if a.dtype == BF16:
        bh, bl = split(b)
        return dot(a, bh, dims) + dot(a, bl, dims)
    ah, al = split(a)
    return dot(ah, b, dims) + dot(al, b, dims)


SLOT = 8


def three_pieces(v):
    hi = v.astype(BF16).astype(F32)
    rest = v - hi
    mid = rest.astype(BF16).astype(F32)
    low = (rest - mid).astype(BF16).astype(F32)
    return hi + pltpu.roll(mid, SLOT, 1) + pltpu.roll(low, 2 * SLOT, 1)


def triangle_sum(mask, v, heads):
    r = dot(jnp.where(mask, 1.0, 0.0).astype(BF16), three_pieces(v).astype(BF16))
    n = r.shape[1]
    r = r + (pltpu.roll(r, n - SLOT, 1) + pltpu.roll(r, n - 2 * SLOT, 1))
    lane = lax.broadcasted_iota(jnp.int32, r.shape, 1)
    return jnp.where(lane < heads, r, 0.0)


def by_channel(cum, step, spread):
    sh, sl = split(step)
    packed = three_pieces(cum) + (
        pltpu.roll(sh.astype(F32), 3 * SLOT, 1) + pltpu.roll(sl.astype(F32), 4 * SLOT, 1)
    )
    both = dot(packed.astype(BF16), spread)
    half = both.shape[1] // 2
    return both[:, :half], both[:, half:]


def sigmoid(v):
    return 1.0 / (1.0 + jnp.exp(-v))


def steps_of(sr, hp, heads):
    lane = lax.broadcasted_iota(jnp.int32, sr.shape, 1)
    moved = sr + hp[0:1]
    step = jnp.maximum(moved, 0.0) + jnp.log1p(jnp.exp(-jnp.abs(moved)))
    step = jnp.where(lane < heads, step, 0.0)
    return moved, step, -step * hp[1:2]


def triangle(q, lower):
    row = lax.broadcasted_iota(jnp.int32, (q, q), 0)
    col = lax.broadcasted_iota(jnp.int32, (q, q), 1)
    return (row >= col) if lower else (col >= row)


def contract_rows(front, rep, ch, width):
    start = rep * (ch // 2)
    if not isinstance(rep, int):
        start = pl.multiple_of(start, 16)
    pair = front[pl.ds(start, ch // 2), front.shape[1] - 2 * width :]
    return jnp.concatenate([pair[:, :width], pair[:, width:]], axis=0)


def beside(ref, parity, value, lead=None):
    half = value.shape[1]
    for odd in (0, 1):

        @pl.when(parity == odd)
        def _():
            if lead is None:
                ref[:, odd * half : odd * half + half] = value
            else:
                ref[lead, :, odd * half : odd * half + half] = value


def pick(out, source, m, near0, near1, near3, far0, far1):
    for index, ref in ((0, near0), (1, near1), (3, near3)):

        @pl.when(source == index)
        def _():
            out[...] = ref[0]

    for micro, ref in enumerate((far0, far1)):

        @pl.when((source == 2) & (m == micro))
        def _():
            out[...] = ref[0]


def forward_kernel(
    heads, reps, place, n0, n1, n3, n2a, n2b, b0, b1, b3, b2a, b2b, front, perm, fp, hp, cp, spread,
    nrm_o, bg_o, gate_o, sig_o, pre_o, y_o, oc_o, sr_o, sin_o, sums_o, pwr_o, swr_o,
    state, tail, co,
):
    q = nrm_o.shape[0]
    ch = cp.shape[1]
    cw = fp.shape[1]
    ns = (cw - ch) // 2
    wr = 2 * ns // reps
    size = ch // heads
    step_id = pl.program_id(0)
    block = step_id % reps
    rep = place[0]
    source = (block - rep + reps) % reps

    pick(nrm_o, source, step_id // reps, n0, n1, n3, n2a, n2b)
    pick(bg_o, source, step_id // reps, b0, b1, b3, b2a, b2b)

    @pl.when(step_id == 0)
    def _():
        co[...] = dot(perm[...], contract_rows(front, rep, ch, nrm_o.shape[1])).astype(BF16)

    @pl.when(block == 0)
    def _():
        state[...] = jnp.zeros_like(state)
        tail[...] = jnp.zeros_like(tail)

    proj = dot(nrm_o[...], front[:, : ch + cw + 128])
    gate = proj[:, :ch]
    signal = proj[:, ch : ch + cw]
    lane = lax.broadcasted_iota(jnp.int32, (q, 128), 1)
    sr = jnp.where(lane < heads, proj[:, ch + cw : ch + cw + 128], 0.0)
    ext = jnp.concatenate([tail[...], signal], axis=0)
    pre = fp[4:5, :] + jnp.zeros_like(signal)
    for k in range(4):
        pre = pre + fp[k : k + 1, :] * ext[5 + k : 5 + k + q]
    tail[...] = signal[q - 8 :]
    act = pre * sigmoid(pre)
    values = act[:, :ch]
    writer = act[:, ch : ch + ns]
    reader = act[:, ch + ns :]
    _, step, ld = steps_of(sr, hp[...], heads)
    lower = triangle(q, True)
    cum = triangle_sum(lower, ld, heads)
    cum_t = cum.T
    cum_e, step_e = by_channel(cum, step, spread[...])
    last_e = cum_e[q - 1 : q]
    xv = step_e * values
    scores = dot3(reader, writer, NT)
    parts = []
    for p in range(ch // 128):
        hi, lo = split(xv[:, 128 * p : 128 * p + 128])
        both = jnp.concatenate([hi, lo], axis=1)
        out = None
        for j in range(128 // size):
            h = p * (128 // size) + j
            decay = jnp.exp(cum[:, h : h + 1] - cum_t[h : h + 1, :])
            ph, plo = split(jnp.where(lower, scores * decay, 0.0))
            r = dot(ph, both)
            one = r[:, :128] + (r[:, 128:] + dot(plo, hi))
            out = one if out is None else jnp.where(lane < j * size, out, one)
        parts.append(out)
    inner = jnp.concatenate(parts, axis=1)
    old = state[...]
    sin_o[0] = old
    y = inner + jnp.exp(cum_e) * dot3(reader, old, NT) + cp[0:1, :] * values
    decay_ch = jnp.broadcast_to(jnp.exp(last_e), (ns, ch)).T
    state[...] = decay_ch * old + dot3(jnp.exp(last_e - cum_e) * xv, writer, TN)
    gated = y * (gate * sigmoid(gate))
    outcome = dot(bg_o[...], co[...], NT)
    ones = jnp.ones((8, ch), BF16)
    s1 = dot2(ones, gated * gated, NT)
    s2 = dot2(ones, outcome * cp[1:2, :] * gated, NT)
    row = lax.broadcasted_iota(jnp.int32, s1.shape, 0)
    both_sums = jnp.where(row == 0, s1, jnp.where(row == 1, s2, 0.0))
    for r in range(reps):
        sums_o[r] = both_sums
    gate_o[...] = gate
    sig_o[...] = signal[:, :ch]
    pre_o[...] = pre
    y_o[...] = y
    oc_o[...] = outcome
    sr_o[...] = sr
    for r in range(reps):

        @pl.when(rep == r)
        def _():
            beside(pwr_o, block % 2, pre[:, ch + r * wr : ch + r * wr + wr])
            beside(swr_o, block % 2, signal[:, ch + r * wr : ch + r * wr + wr])


def gate_kernel(
    width, ys, gate_r, y_r, oc_r, sums, bg, nrm, cp, send_o, early_o, dy_o, acc_o, cg
):
    q, ch = gate_r.shape
    dp = early_o.shape[0]
    rows = nrm.shape[1] // dp
    piece = (early_o.shape[1] - rows) // 2

    @pl.when(pl.program_id(0) == 0)
    def _():
        cg[...] = jnp.zeros_like(cg)
        early_o[...] = jnp.zeros_like(early_o)
        acc_o[...] = jnp.zeros_like(acc_o)

    s = jnp.sum(sums[...], axis=0)
    scale_row = lax.rsqrt(s[0:1] * (1.0 / width) + EPS)
    mean_row = scale_row * s[1:2] * (1.0 / width)

    def column(v):
        c = jnp.broadcast_to(v, (128, q)).T
        return jnp.concatenate([c] * (ch // 128), axis=1)

    scale = column(scale_row)
    mean = column(mean_row)
    gate = gate_r[...]
    y = y_r[...]
    outcome = oc_r[...]
    gain = cp[1:2, :]
    sg = sigmoid(gate)
    sl = gate * sg
    unit = y * sl * scale
    nout = (unit * gain).astype(BF16)
    cg[...] += dot(nout, bg[...], TN)
    gated_grad = scale * (outcome * gain - unit * mean)
    dy_o[...] = gated_grad * sl
    gg = (gated_grad * y * sg * (1.0 + gate * (1.0 - sg))).astype(BF16)
    early_o[:, :rows, :] += dot(nrm[...], gg, TN).reshape(dp, rows, ch)
    send_o[0, :, :ch] = nout
    send_o[0, :, ch:] = gg
    gain_part = jnp.sum(outcome * unit, axis=0, keepdims=True)
    row = lax.broadcasted_iota(jnp.int32, acc_o.shape, 0)
    acc_o[...] += jnp.where(row == 0, gain_part, 0.0)

    @pl.when(pl.program_id(0) == pl.num_programs(0) - 1)
    def _():
        half = bg.shape[1] // 2
        for d in range(dp):
            start = (d % (dp // ys)) * ys * piece + (d // (dp // ys)) * piece
            part = cg[start : start + piece, :]
            early_o[d, rows : rows + piece, :] = part[:, :half]
            early_o[d, rows + piece :, :] = part[:, half:]


def backward_kernel(
    heads, reps, sig_r, pre_r, y_r, dy_r, sr_r, sin_r, fp, hp, cp, spread, oh,
    vg_o, send_o, wr_o, raw_o, acc_o, hacc_o,
    adj, head_rows,
):
    q, ch = y_r.shape
    cw = fp.shape[1]
    ns = (cw - ch) // 2
    wr = 2 * ns // reps
    size = ch // heads
    block = reps - 1 - pl.program_id(0) % reps

    @pl.when(block == reps - 1)
    def _():
        adj[...] = jnp.zeros_like(adj)
        head_rows[...] = jnp.zeros_like(head_rows)

    @pl.when(pl.program_id(0) == 0)
    def _():
        acc_o[...] = jnp.zeros_like(acc_o)
        hacc_o[...] = jnp.zeros_like(hacc_o)

    pre = pre_r[...]
    sgm = sigmoid(pre)
    act = pre * sgm
    values = act[:, :ch]
    writer = act[:, ch : ch + ns]
    reader = act[:, ch + ns :]
    moved_raw, step, ld = steps_of(sr_r[...], hp[...], heads)
    lower = triangle(q, True)
    upper = triangle(q, False)
    cum = triangle_sum(lower, ld, heads)
    cum_t = cum.T
    cum_e, step_e = by_channel(cum, step, spread[...])
    last_e = cum_e[q - 1 : q]
    skip = cp[0:1, :]
    dy = dy_r[...]
    y = y_r[...]
    xv = step_e * values
    lane = lax.broadcasted_iota(jnp.int32, (q, 128), 1)
    scores = dot3(writer, reader, NT)
    dscores = jnp.zeros((q, q), F32)
    parts = []
    for p in range(ch // 128):
        dpair = dy[:, 128 * p : 128 * p + 128]
        xpair = xv[:, 128 * p : 128 * p + 128]
        dh, dl = split(dpair)
        dboth = jnp.concatenate([dh, dl], axis=1)
        dtwice = jnp.concatenate([dh, dh], axis=1)
        out = None
        for j in range(128 // size):
            h = p * (128 // size) + j
            decay = jnp.where(upper, jnp.exp(cum_t[h : h + 1, :] - cum[:, h : h + 1]), 0.0)
            ph, plo = split(scores * decay)
            r = dot(ph, dboth)
            one = r[:, :128] + (r[:, 128:] + dot(plo, dh))
            out = one if out is None else jnp.where(lane < j * size, out, one)
            mine = (lane >= j * size) & (lane < (j + 1) * size)
            xh, xl = split(jnp.where(mine, xpair, 0.0))
            m = dot(jnp.concatenate([xh, xl], axis=1), dtwice, NT) + dot(xh, dl, NT)
            dscores = dscores + m * decay
        parts.append(out)
    inner = jnp.concatenate(parts, axis=1)
    old = adj[...]
    sin = sin_r[0]
    ends = jnp.exp(last_e - cum_e)
    from_state = ends * dot3(writer, old, NT)
    dxv = inner + from_state
    cdy = jnp.exp(cum_e) * dy
    dwriter = dot3(dscores, reader) + dot3(ends * xv, old)
    dreader = dot3(dscores, writer, TN) + dot3(cdy, sin)
    decay_ch = jnp.broadcast_to(jnp.exp(last_e), (ns, ch)).T
    state_row = dot2(jnp.ones((8, ns), BF16), decay_ch * old * sin, NT)[0:1]
    last_row = state_row + jnp.sum(xv * from_state, axis=0, keepdims=True)
    adj[...] = decay_ch * old + dot3(cdy, reader, TN)

    dstep = dot2(values * dxv, oh[...], NT)
    row = lax.broadcasted_iota(jnp.int32, (q, ch), 0)
    dcum_ch = dy * (y - skip * values) - xv * dxv + jnp.where(row == q - 1, last_row, 0.0)
    dcum = dot2(dcum_ch, oh[...], NT)
    dld = triangle_sum(upper, dcum, heads)
    raw = (dstep - dld * hp[1:2]) * sigmoid(moved_raw)
    raw = jnp.where(lane < heads, raw, 0.0)
    raw_o[...] = jnp.concatenate([jnp.zeros((q, wr), F32), raw[:, : 128 - wr]], axis=1)
    hrow = lax.broadcasted_iota(jnp.int32, hacc_o.shape, 0)
    hacc_o[...] += jnp.where(
        hrow == 0,
        jnp.sum(raw, axis=0, keepdims=True),
        jnp.where(hrow == 1, jnp.sum(dld * ld, axis=0, keepdims=True), 0.0),
    )
    both = jnp.concatenate([dwriter, dreader], axis=1)
    for r in range(reps):
        beside(wr_o, block % 2, both[:, r * wr : r * wr + wr], r)

    sv = sgm[:, :ch]
    dpre = (step_e * dxv + skip * dy) * (sv * (1.0 + pre[:, :ch] * (1.0 - sv)))
    ext = jnp.concatenate([dpre, head_rows[...]], axis=0)
    head_rows[...] = dpre[:8]
    signal = sig_r[...]
    total = jnp.zeros_like(dpre)
    rows = []
    for k in range(4):
        moved = ext[3 - k : 3 - k + q]
        total = total + fp[k : k + 1, :ch] * moved
        rows.append(jnp.sum(moved * signal, axis=0, keepdims=True))
    vg = total.astype(BF16)
    vg_o[...] = vg
    send_o[0] = vg
    rows.append(jnp.sum(dpre, axis=0, keepdims=True))
    rows.append(jnp.sum(values * dy, axis=0, keepdims=True))
    rows.append(jnp.zeros((2, ch), F32))
    acc_o[...] += jnp.concatenate(rows, axis=0)


def tail_kernel(wr, got, pwr, swr, fw, raw, tail_o, send_o, acc_o):
    half = got.shape[1] // 2

    def line(v):
        return jnp.concatenate(
            [v[:half, :wr], v[:half, wr:], v[half:, :wr], v[half:, wr:]], axis=0
        )

    pre = pwr[...]
    s = sigmoid(pre)
    grads = jnp.sum(got[...], axis=0)
    dpre = line(grads * (s * (1.0 + pre * (1.0 - s))))
    signal = line(swr[...])
    total = jnp.zeros_like(dpre)
    ext = jnp.concatenate([dpre, jnp.zeros((8, wr), F32)], axis=0)
    rows = []
    n = dpre.shape[0]
    for k in range(4):
        moved = ext[3 - k : 3 - k + n]
        total = total + fw[k : k + 1, :] * moved
        rows.append(jnp.sum(moved * signal, axis=0, keepdims=True))
    rows.append(jnp.sum(dpre, axis=0, keepdims=True))
    rows.append(jnp.zeros((3, wr), F32))

    @pl.when(pl.program_id(0) == 0)
    def _():
        acc_o[...] = jnp.zeros_like(acc_o)

    acc_o[...] += jnp.concatenate(rows, axis=0)
    wide = jnp.concatenate([total, jnp.zeros((n, 128 - wr), F32)], axis=1)
    tail = (wide + raw[...]).astype(BF16)
    tail_o[...] = tail
    send_o[...] = tail.reshape(send_o.shape)


def mix_kernel(parts, front, perm, mask, residual, out):
    micro, q, width = residual.shape
    ch = perm.shape[0]
    totals = [0.0] * micro
    for k in range(parts.shape[0]):
        rows = contract_rows(front, k, ch, width)
        for m in range(micro):
            moved = dot(parts[k, :, 2 * m * ch : (2 * m + 1) * ch], perm[...]).astype(BF16)
            totals[m] = totals[m] + dot(moved, rows)
    for m in range(micro):
        out[m] = residual[m] + mask[m] * totals[m]


def first_kernel(parts, expand, out):
    micro = out.shape[0]
    reps = parts.shape[0]
    span = expand.shape[1] // reps
    ch = (span - 128) // 2
    totals = [0.0] * micro
    for k in range(reps):
        cols = expand[:, k * span : k * span + ch]
        for m in range(micro):
            totals[m] = totals[m] + dot(parts[k, :, (2 * m + 1) * ch : (2 * m + 2) * ch], cols, NT)
    for m in range(micro):
        out[m] = totals[m]


def last_kernel(part, parts, expand, residual, cotangent, gain, out, norm_o):
    micro, q, width = residual.shape
    reps = parts.shape[0]
    span = expand.shape[1] // reps
    ch = (span - 128) // 2
    totals = [part[m] for m in range(micro)]
    for k in range(reps):
        cols = expand[:, k * span + ch : (k + 1) * span]
        for m in range(micro):
            at = micro * ch + m * 128
            pg = jnp.concatenate([parts[k, :, m * ch : (m + 1) * ch], parts[k, :, at : at + 128]], axis=1)
            totals[m] = totals[m] + dot(pg, cols, NT)
    norm = jnp.zeros((1, width), F32)
    for m in range(micro):
        source = residual[m]
        scale = lax.rsqrt(jnp.mean(source * source, axis=-1, keepdims=True) + EPS)
        unit = source * scale
        norm = norm + jnp.sum(totals[m] * unit, axis=0, keepdims=True)
        scaled = totals[m] * gain[0:1]
        out[m] = cotangent[m] + scale * (
            scaled - unit * jnp.mean(scaled * unit, axis=-1, keepdims=True)
        )
    norm_o[...] = jnp.broadcast_to(norm, norm_o.shape)


def whole(shape):
    return pl.BlockSpec(shape, lambda *b: (0,) * len(shape))


def rows_of(q, width, order=lambda b: b):
    return pl.BlockSpec((q, width), lambda b: (order(b), 0))


SCALAR = pl.BlockSpec(memory_space=pltpu.SMEM)


def params(flops, nbytes, grid=True):
    kinds = dict(dimension_semantics=("arbitrary",)) if grid else {}
    return dict(
        compiler_params=pltpu.CompilerParams(vmem_limit_bytes=VMEM_LIMIT, **kinds),
        cost_estimate=pl.CostEstimate(flops=flops, bytes_accessed=nbytes, transcendentals=0),
    )


def body(
    dims,
    residual, lengths, norm_gain, expand, filters, offsets, gate_gain, contract,
    step_bias, decay_log, skip_gain, cotangent,
):
    ax = Axes(dims)
    micro, _, q, width = residual.shape
    heads_all = step_bias.shape[0]
    reps = lax.axis_size("rep")
    heads = heads_all // reps
    dp = lax.axis_size("dp")
    inner = contract.shape[0] * dp
    ch = inner // reps
    conv = filters.shape[0] * dp
    ns = (conv - inner) // 2
    cw = ch + 2 * ns
    size = inner // heads_all
    total = q * reps
    rep = lax.axis_index("rep")
    rows = expand.shape[0]
    wr = 2 * ns // reps
    sds = jax.ShapeDtypeStruct
    residual = residual[:, 0]
    cotangent = cotangent[:, 0]
    place = rep.astype(jnp.int32).reshape(1)

    def own(a, start, count, dim=-1):
        return lax.dynamic_slice_in_dim(a, start + rep * count, count, a.ndim + dim)

    position = rep * q + jnp.arange(q, dtype=jnp.int32)
    mask = (position[None, :] < lengths[:, :1]).astype(F32)[..., None]
    branch_grad = (mask * cotangent).astype(BF16)

    branch_grad, expand, contract = lax.optimization_barrier((branch_grad, expand, contract))

    half = contract.shape[0] // 2
    front = jnp.concatenate(
        [
            own(expand, 0, ch),
            own(expand, inner, ch),
            expand[:, 2 * inner : 2 * inner + 2 * ns],
            jnp.pad(own(expand, 2 * inner + 2 * ns, heads), ((0, 0), (0, 128 - heads))),
            contract[:half],
            contract[half:],
        ],
        axis=1,
    )
    w_width = ch + cw + 128
    with jax.named_scope("gather_own_expand"):
        front = lax.all_gather(front, "dp", axis=0, tiled=True)
    order = np.arange(ch).reshape(-1, 2, half).transpose(1, 0, 2).reshape(-1)
    perm = np.zeros((ch, ch), np.float32)
    perm[order, np.arange(ch)] = 1.0
    perm = jnp.asarray(perm, BF16)
    small = jnp.concatenate([norm_gain, filters.reshape(-1), offsets, gate_gain])
    sizes = np.cumsum([0, norm_gain.shape[0], filters.size, offsets.shape[0], gate_gain.shape[0]])
    padded = -(-small.shape[0] // 128) * 128
    small = jnp.pad(small, (0, padded - small.shape[0])).reshape(-1, 128)
    with jax.named_scope("gather_small"):
        small, branch_grad = lax.optimization_barrier((small, branch_grad))
        small = jnp.broadcast_to(small[None], (dp,) + small.shape)
        small = lax.all_to_all(small, "dp", 0, 0, tiled=True).reshape(dp, padded).astype(F32)
    with jax.named_scope("gather_branch_grad"):
        bg_near = ax.near_ring(branch_grad)
    gain_one = small[:, sizes[0] : sizes[1]].reshape(1, width)
    filters_full = small[:, sizes[1] : sizes[2]].reshape(conv, 4).T
    offsets_full = small[:, sizes[2] : sizes[3]].reshape(1, conv)
    gain_two = small[:, sizes[3] : sizes[4]].reshape(1, inner)

    scale_one = lax.rsqrt(jnp.mean(residual * residual, axis=-1, keepdims=True) + EPS)
    normed = (residual * scale_one * gain_one).astype(BF16)
    normed, expand, bg_near = lax.optimization_barrier((normed, expand, bg_near))
    with jax.named_scope("gather_normed"):
        nrm_ring = ax.far_ring(normed, *ax.near_ring(normed))
    with jax.named_scope("gather_branch_grad"):
        bg_ring = ax.far_ring(branch_grad, *bg_near)
    expand_cols = jnp.concatenate(
        [
            expand[:, :inner].reshape(rows, reps, ch),
            expand[:, inner : 2 * inner].reshape(rows, reps, ch),
            expand[:, 2 * inner : 2 * inner + 2 * ns].reshape(rows, reps, wr),
            expand[:, 2 * inner + 2 * ns :].reshape(rows, reps, heads),
            jnp.zeros((rows, reps, 128 - wr - heads), BF16),
        ],
        axis=2,
    ).reshape(rows, reps * (2 * ch + 128))
    with jax.named_scope("gather_expand"):
        expand_full = lax.all_gather(expand_cols, "dp", axis=0, tiled=True)

    own_filters = jnp.concatenate(
        [own(filters_full[:, :inner], 0, ch), filters_full[:, inner:]], axis=1
    )
    own_offsets = jnp.concatenate(
        [own(offsets_full[:, :inner], 0, ch), offsets_full[:, inner:]], axis=1
    )
    fp = jnp.concatenate([own_filters, own_offsets, jnp.zeros((3, cw), F32)], axis=0)
    own_skip = own(skip_gain, 0, heads)
    cp = jnp.concatenate(
        [jnp.repeat(own_skip, size)[None], own(gain_two, 0, ch), jnp.zeros((6, ch), F32)], axis=0
    )
    rate = jnp.exp(own(decay_log, 0, heads))
    hp = jnp.pad(jnp.stack([own(step_bias, 0, heads), rate]), ((0, 6), (0, 128 - heads)))
    onehot = np.zeros((128, ch), np.float32)
    onehot[np.arange(ch) // size, np.arange(ch)] = 1.0
    spread_of = np.zeros((128, 2 * ch), np.float32)
    for piece in range(5):
        spread_of[piece * SLOT : (piece + 1) * SLOT, (piece // 3) * ch : (piece // 3 + 1) * ch] = onehot[:SLOT]
    onehot = jnp.asarray(onehot, BF16)
    spread_of = jnp.asarray(spread_of, BF16)

    piece = pl.BlockSpec((1, q, width), lambda b: (b // reps, 0, 0))
    ring_specs = [piece, piece, piece, whole((1, q, width)), whole((1, q, width))]
    both = micro * total
    aside = pl.BlockSpec((q, 128), lambda b: (b // 2, 0))
    kept = pl.pallas_call(
        functools.partial(forward_kernel, heads, reps),
        grid=(micro * reps,),
        in_specs=[SCALAR] + ring_specs * 2 + [
            whole(front.shape), whole((ch, ch)),
            whole((8, cw)), whole((8, 128)), whole((8, ch)), whole((128, 2 * ch)),
        ],
        out_specs=[
            rows_of(q, width), rows_of(q, width),
            rows_of(q, ch), rows_of(q, ch), rows_of(q, cw), rows_of(q, ch), rows_of(q, ch),
            rows_of(q, 128), pl.BlockSpec((1, ch, ns), lambda b: (b, 0, 0)),
            pl.BlockSpec((reps, 8, q), lambda b: (0, 0, b)), aside, aside,
        ],
        out_shape=[
            sds((both, width), BF16), sds((both, width), BF16),
            sds((both, ch), F32), sds((both, ch), F32), sds((both, cw), F32),
            sds((both, ch), F32), sds((both, ch), F32), sds((both, 128), F32),
            sds((micro * reps, ch, ns), F32), sds((reps, 8, both), F32),
            sds((both // 2, 2 * wr), F32), sds((both // 2, 2 * wr), F32),
        ],
        scratch_shapes=[
            pltpu.VMEM((ch, ns), F32), pltpu.VMEM((8, cw), F32), pltpu.VMEM((ch, width), BF16),
        ],
        name="scan_forward",
        **params(40_000_000_000, 40_000_000),
    )(place, *nrm_ring, *bg_ring, front, perm, fp, hp, cp, spread_of)
    nrm, bg, gate, signal, pre, y, outcome, sr, sin, sums, pwr, swr = kept
    with jax.named_scope("sum_norm_terms"):
        sums, expand_full = lax.optimization_barrier((ax.exchange(sums), expand_full))

    strip = pl.BlockSpec((reps, 8, q), lambda b: (0, 0, b))
    ys = ax.size["y"]
    wide = width // 2
    early_rows = rows + 2 * (contract.shape[0] // ys)
    send, early, dy, gain_part = pl.pallas_call(
        functools.partial(gate_kernel, inner, ys),
        grid=(micro * reps,),
        in_specs=[rows_of(q, ch)] * 3 + [strip] + [rows_of(q, width)] * 2 + [whole((8, ch))],
        out_specs=[
            pl.BlockSpec((1, q, 2 * ch), lambda b: (b % reps, 0, b // reps)),
            whole((dp, early_rows, ch)), rows_of(q, ch), whole((8, ch)),
        ],
        out_shape=[
            sds((reps, q, micro * 2 * ch), BF16), sds((dp, early_rows, ch), F32),
            sds((both, ch), F32), sds((8, ch), F32),
        ],
        scratch_shapes=[pltpu.VMEM((ch, width), F32)],
        name="gate_backward",
        **params(8_000_000_000, 20_000_000),
    )(gate, y, outcome, sums, bg, nrm, cp)
    with jax.named_scope("early_sums"):
        early = lax.psum_scatter(early, "dp", scatter_dimension=0)

    with jax.named_scope("send_gate_parts"):
        a_parts = ax.exchange(send)
    def back(b):
        return b // reps * reps + reps - 1 - b % reps

    value_grads, v_send, wrg, raws, channel_part, head_part = pl.pallas_call(
        functools.partial(backward_kernel, heads, reps),
        grid=(micro * reps,),
        in_specs=[
            rows_of(q, ch, back), rows_of(q, cw, back), rows_of(q, ch, back), rows_of(q, ch, back),
            rows_of(q, 128, back), pl.BlockSpec((1, ch, ns), lambda b: (back(b), 0, 0)),
            whole((8, cw)), whole((8, 128)), whole((8, ch)), whole((128, 2 * ch)), whole((128, ch)),
        ],
        out_specs=[
            rows_of(q, ch, back),
            pl.BlockSpec((1, q, ch), lambda b: (back(b) % reps, 0, b // reps)),
            pl.BlockSpec((reps, q, 2 * wr), lambda b: (0, back(b) // 2, 0)),
            rows_of(q, 128, back), whole((8, ch)), whole((8, 128)),
        ],
        out_shape=[
            sds((both, ch), BF16), sds((reps, q, micro * ch), BF16),
            sds((reps, both // 2, 2 * wr), F32),
            sds((both, 128), F32), sds((8, ch), F32), sds((8, 128), F32),
        ],
        scratch_shapes=[pltpu.VMEM((ch, ns), F32), pltpu.VMEM((8, ch), F32)],
        name="scan_backward",
        **params(80_000_000_000, 40_000_000),
    )(signal, pre, y, dy, sr, sin, fp, hp, cp, spread_of, onehot)
    with jax.named_scope("sum_writer_reader_grad"):
        a_parts, wrg = lax.optimization_barrier((a_parts, wrg))
        wr_got = ax.exchange(wrg)
    vmem = pl.BlockSpec(memory_space=pltpu.VMEM)
    mixed = pl.pallas_call(
        mix_kernel,
        in_specs=[vmem] * 5,
        out_specs=vmem,
        out_shape=sds(residual.shape, F32),
        name="mixed",
        **params(1_200_000_000, 8_000_000, False),
    )(a_parts, front, perm, mask, residual)
    first = pl.pallas_call(
        first_kernel,
        in_specs=[vmem] * 2,
        out_specs=vmem,
        out_shape=sds(residual.shape, F32),
        name="normed_grad_gate",
        **params(1_200_000_000, 8_000_000, False),
    )(a_parts, expand_full)
    with jax.named_scope("late_sums"):
        eg_values = lax.dot_general(nrm, value_grads, TN, preferred_element_type=F32)
    first, mixed, eg_values, wr_got = lax.optimization_barrier((first, mixed, eg_values, wr_got))
    fw = jnp.pad(own(filters_full[:, inner:], 0, wr), ((0, 4), (0, 0)))
    strip = pl.BlockSpec((total // 2, 2 * wr), lambda m: (m, 0))
    tails, t_send, wr_part = pl.pallas_call(
        functools.partial(tail_kernel, wr),
        grid=(micro,),
        in_specs=[
            pl.BlockSpec((reps, total // 2, 2 * wr), lambda m: (0, m, 0)), strip, strip,
            whole((8, wr)), rows_of(total, 128),
        ],
        out_specs=[
            rows_of(total, 128), pl.BlockSpec((reps, q, 128), lambda m: (0, 0, m)), whole((8, wr)),
        ],
        out_shape=[
            sds((both, 128), BF16), sds((reps, q, micro * 128), BF16), sds((8, wr), F32),
        ],
        name="writer_reader_grad",
        **params(100_000_000, 6_000_000),
    )(wr_got, pwr, swr, fw, raws)
    with jax.named_scope("send_values"):
        v_parts = ax.exchange(jnp.concatenate([v_send, t_send], axis=2))

    def spread(a, whole_width):
        blank = jnp.zeros((a.shape[0], whole_width), F32)
        return lax.dynamic_update_slice_in_dim(blank, a, rep * a.shape[1], 1)

    with jax.named_scope("late_sums"):
        taps = jnp.concatenate([spread(channel_part[:5], inner), spread(wr_part[:5], 2 * ns)], axis=1)
        own_heads = jnp.stack(
            [
                head_part[0, :heads],
                head_part[1, :heads],
                jnp.sum(channel_part[5].reshape(heads, size), axis=1),
            ]
        )
        heads_part = jnp.broadcast_to(spread(own_heads, heads_all).reshape(1, -1), (dp, 3 * heads_all))
        per = conv // dp
        flat = jnp.concatenate(
            [
                jnp.transpose(taps.reshape(5, dp, per), (1, 0, 2)).reshape(dp, 5 * per),
                spread(gain_part[:1], inner).reshape(dp, -1),
                heads_part,
            ],
            axis=1,
        )
        cuts = np.cumsum([0, 5 * per, inner // dp, 3 * heads_all])
        block = ch + 128
        spare = 56
        flat = jnp.pad(flat, ((0, 0), (0, rows * spare - flat.shape[1]))).reshape(dp, rows, spare)
        flat = jnp.pad(flat, ((0, 0), (0, 0), (128 - spare, 0)))
        eg_tail = lax.dot_general(nrm, tails, TN, preferred_element_type=F32)
        early, eg_tail = lax.optimization_barrier((early, eg_tail))
        late = jnp.concatenate(
            [eg_values.reshape(dp, rows, ch), eg_tail.reshape(dp, rows, 128) + flat], axis=2
        )
        late = late.reshape(dims + late.shape[1:])
        late = ax.scatter_sum(late, "core", 2)
        late = ax.scatter_sum(late, "x", 1)
        late = ax.scatter_sum(late, "y", 0)
    with jax.named_scope("last_gather"):
        late, v_parts = lax.optimization_barrier((late, v_parts))
        eg_gate = early[:rows]
        cgs = early[rows:]
        if ys == reps:
            turn = [(a * (dp // ys) + e) * reps + b for a in range(ys) for e in range(dp // ys) for b in range(reps)]
            to = [(b * (dp // ys) + e) * reps + a for a in range(ys) for e in range(dp // ys) for b in range(reps)]
            cgs = lax.ppermute(cgs, ("dp", "rep"), list(zip(turn, to)))
        packed = jnp.concatenate([eg_gate.reshape(-1, 128), cgs.reshape(-1, 128), late.reshape(-1, 128)], axis=0)
    residual_grad, norm_part = pl.pallas_call(
        last_kernel,
        in_specs=[vmem] * 6,
        out_specs=[vmem] * 2,
        out_shape=[sds(residual.shape, F32), sds((8, width), F32)],
        name="residual_grad",
        **params(2_000_000_000, 15_000_000, False),
    )(first, v_parts, expand_full, residual, cotangent, gain_one)
    with jax.named_scope("sum_norm_grad"):
        spread_norm = norm_part[:1].reshape(dp, 1, -1)
        spread_norm = jnp.pad(spread_norm, ((0, 0), (0, 0), (0, -spread_norm.shape[2] % 128)))
        norm_sum = jnp.sum(lax.all_to_all(spread_norm, "dp", 0, 0, tiled=True), axis=0)
        norm_sum = jnp.pad(norm_sum.reshape(-1, 128), ((0, -norm_sum.size // 128 % 8), (0, 0)))
    with jax.named_scope("last_gather"):
        got = ax.everywhere(jnp.concatenate([packed, norm_sum], axis=0))
    mark = rows * ch // 128
    eg_gate = got[:, :mark].reshape(reps, rows, ch)
    cgs = got[:, mark : 2 * mark].reshape(reps, 2, -1, wide)
    late = got[:, 2 * mark : packed.shape[0]].reshape(reps, rows, block)
    norm_grad = jnp.sum(got[:, packed.shape[0] :], axis=0).reshape(-1)[: width // dp]
    contract_grad = jnp.concatenate([cgs[:, 0], cgs[:, 1]], axis=2).reshape(-1, width)
    expand_grad = jnp.concatenate(
        [eg_gate[s] for s in range(reps)]
        + [late[s, :rows, :ch] for s in range(reps)]
        + [late[s, :rows, ch : ch + wr] for s in range(reps)]
        + [late[s, :rows, ch + wr : ch + wr + heads] for s in range(reps)],
        axis=1,
    )
    flat = jnp.sum(late[:, :, block - spare :], axis=0).reshape(-1)
    own_taps = flat[: cuts[1]].reshape(5, per)
    gain_grad = flat[cuts[1] : cuts[2]]
    by_head = flat[cuts[2] : cuts[3]].reshape(3, heads_all)
    return (
        mixed[:, None],
        residual_grad[:, None],
        norm_grad,
        expand_grad,
        own_taps[:4].T,
        own_taps[4],
        gain_grad,
        contract_grad,
        by_head[0],
        by_head[1],
        by_head[2],
    )


def solution(mesh):
    dp, rep = mesh.devices.shape
    core = 2 if dp % 8 == 0 else 1
    dims = (rep, dp // (core * rep), core)
    rows = P(None, "dp", "rep", None)
    in_specs = (
        rows, P(None, "dp"), P("dp"), P("dp", None), P("dp", None), P("dp"), P("dp"), P("dp", None),
        P(), P(), P(), rows,
    )
    out_specs = (
        rows, rows, P("dp"), P("dp", None), P("dp", None), P("dp"), P("dp"), P("dp", None),
        P(), P(), P(),
    )
    return jax.shard_map(
        functools.partial(body, dims), mesh=mesh, in_specs=in_specs, out_specs=out_specs, check_vma=False
    )
```

```python
import functools

import jax
import jax.numpy as jnp
import numpy as np
from jax import lax
from jax.experimental import pallas as pl
from jax.experimental.pallas import tpu as pltpu
from jax.sharding import PartitionSpec as P

EPS = 1e-05
F32 = jnp.float32
BF16 = jnp.bfloat16
NN = (((1,), (0,)), ((), ()))
NT = (((1,), (1,)), ((), ()))
TN = (((0,), (0,)), ((), ()))
VMEM_LIMIT = 56 * 1024 * 1024


class Axes:
    def __init__(self, dims):
        self.size = dict(zip(("y", "x", "core"), dims))
        place = lax.axis_index("dp")
        y, x, core = dims
        self.place = {
            "y": place // (x * core),
            "x": (place // core) % x,
            "core": place % core,
            "rep": lax.axis_index("rep"),
        }
        self.size["rep"] = lax.axis_size("rep")

    def shift(self, v, axis, by):
        n = self.size[axis]
        if axis == "rep":
            return lax.ppermute(v, "rep", [(i, (i + by) % n) for i in range(n)])
        stride = {"core": 1, "x": self.size["core"], "y": self.size["core"] * self.size["x"]}[axis]
        route = []
        for i in range(lax.axis_size("dp")):
            at = (i // stride) % n
            route.append((i, i + ((at + by) % n - at) * stride))
        return lax.ppermute(v, "dp", route)

    def near_ring(self, v):
        return self.shift(v, "rep", 1), self.shift(v, "rep", -1)

    def far_ring(self, v, left, right):
        far = (self.shift(left[:1], "rep", 1), self.shift(right[1:], "rep", -1))
        return [v, right, left, far[0], far[1]]

    def exchange(self, v, axis="rep"):
        n = self.size[axis]
        if n == 1:
            return v
        if axis == "rep":
            return lax.all_to_all(v, "rep", 0, 0, tiled=True)
        stride = {"core": 1, "x": self.size["core"], "y": self.size["core"] * self.size["x"]}[axis]
        starts = [i for i in range(lax.axis_size("dp")) if (i // stride) % n == 0]
        groups = [[i + k * stride for k in range(n)] for i in starts]
        return lax.all_to_all(v, "dp", 0, 0, axis_index_groups=groups, tiled=True)

    def everywhere(self, v, axis="rep"):
        return self.exchange(jnp.broadcast_to(v[None], (self.size[axis],) + v.shape), axis)

    def block(self, v, axis, ahead, dim):
        index = (self.place[axis] + ahead) % self.size[axis]
        return lax.dynamic_index_in_dim(v, index, dim, keepdims=False)

    def scatter_sum(self, v, axis, dim):
        total = self.block(v, axis, 0, dim)
        for k in range(1, self.size[axis]):
            total = total + self.shift(self.block(v, axis, k, dim), axis, k)
        return total


def dot(a, b, dims=NN):
    return lax.dot_general(a, b, dims, preferred_element_type=F32)


def split(a):
    hi = a.astype(BF16)
    return hi, (a - hi.astype(F32)).astype(BF16)


def dot3(a, b, dims=NN):
    ah, al = split(a)
    bh, bl = split(b)
    return dot(ah, bh, dims) + (dot(ah, bl, dims) + dot(al, bh, dims))


def dot2(a, b, dims=NN):
    if a.dtype == BF16:
        bh, bl = split(b)
        return dot(a, bh, dims) + dot(a, bl, dims)
    ah, al = split(a)
    return dot(ah, b, dims) + dot(al, b, dims)


SLOT = 8


def three_pieces(v):
    hi = v.astype(BF16).astype(F32)
    rest = v - hi
    mid = rest.astype(BF16).astype(F32)
    low = (rest - mid).astype(BF16).astype(F32)
    return hi + pltpu.roll(mid, SLOT, 1) + pltpu.roll(low, 2 * SLOT, 1)


def triangle_sum(mask, v, heads):
    r = dot(jnp.where(mask, 1.0, 0.0).astype(BF16), three_pieces(v).astype(BF16))
    n = r.shape[1]
    r = r + (pltpu.roll(r, n - SLOT, 1) + pltpu.roll(r, n - 2 * SLOT, 1))
    lane = lax.broadcasted_iota(jnp.int32, r.shape, 1)
    return jnp.where(lane < heads, r, 0.0)


def by_channel(cum, step, spread):
    sh, sl = split(step)
    packed = three_pieces(cum) + (
        pltpu.roll(sh.astype(F32), 3 * SLOT, 1) + pltpu.roll(sl.astype(F32), 4 * SLOT, 1)
    )
    both = dot(packed.astype(BF16), spread)
    half = both.shape[1] // 2
    return both[:, :half], both[:, half:]


def sigmoid(v):
    return 1.0 / (1.0 + jnp.exp(-v))


def steps_of(sr, hp, heads):
    lane = lax.broadcasted_iota(jnp.int32, sr.shape, 1)
    moved = sr + hp[0:1]
    step = jnp.maximum(moved, 0.0) + jnp.log1p(jnp.exp(-jnp.abs(moved)))
    step = jnp.where(lane < heads, step, 0.0)
    return moved, step, -step * hp[1:2]


def triangle(q, lower):
    row = lax.broadcasted_iota(jnp.int32, (q, q), 0)
    col = lax.broadcasted_iota(jnp.int32, (q, q), 1)
    return (row >= col) if lower else (col >= row)


def contract_rows(front, rep, ch, width):
    start = rep * (ch // 2)
    if not isinstance(rep, int):
        start = pl.multiple_of(start, 16)
    pair = front[pl.ds(start, ch // 2), front.shape[1] - 2 * width :]
    return jnp.concatenate([pair[:, :width], pair[:, width:]], axis=0)


def beside(ref, parity, value, *lead):
    half = value.shape[1]
    for odd in (0, 1):

        @pl.when(parity == odd)
        def _():
            ref[(*lead, slice(None), slice(odd * half, odd * half + half))] = value


def pick(out, source, near0, near1, near3, far0, far1):
    for index, ref in ((0, near0), (1, near1), (3, near3)):

        @pl.when(source == index)
        def _():
            out[...] = ref[...]

    @pl.when(source == 2)
    def _():
        out[0] = far0[0]
        out[1] = far1[0]


def side_by_side(works):
    for _ in zip(*works):
        pass


def forward_kernel(
    heads, reps, place, n0, n1, n3, n2a, n2b, b0, b1, b3, b2a, b2b, front, perm, fp, hp, cp, spread,
    nrm_o, bg_o, gate_o, sig_o, pre_o, y_o, oc_o, sr_o, sin_o, sums_o, pwr_o, swr_o,
    state, tail, co,
):
    micro, q = nrm_o.shape[:2]
    ch = cp.shape[1]
    cw = fp.shape[1]
    ns = (cw - ch) // 2
    wr = 2 * ns // reps
    size = ch // heads
    block = pl.program_id(0)
    rep = place[0]
    source = (block - rep + reps) % reps

    pick(nrm_o, source, n0, n1, n3, n2a, n2b)
    pick(bg_o, source, b0, b1, b3, b2a, b2b)

    @pl.when(block == 0)
    def _():
        co[...] = dot(perm[...], contract_rows(front, rep, ch, nrm_o.shape[2])).astype(BF16)
        state[...] = jnp.zeros_like(state)
        tail[...] = jnp.zeros_like(tail)

    aside = [None] * micro
    lane = lax.broadcasted_iota(jnp.int32, (q, 128), 1)
    lower = triangle(q, True)

    def work(m):
        proj = dot(nrm_o[m], front[:, : ch + cw + 128])
        gate = proj[:, :ch]
        signal = proj[:, ch : ch + cw]
        sr = jnp.where(lane < heads, proj[:, ch + cw : ch + cw + 128], 0.0)
        ext = jnp.concatenate([tail[m], signal], axis=0)
        pre = fp[4:5, :] + jnp.zeros_like(signal)
        for k in range(4):
            pre = pre + fp[k : k + 1, :] * ext[5 + k : 5 + k + q]
        tail[m] = signal[q - 8 :]
        yield
        act = pre * sigmoid(pre)
        values = act[:, :ch]
        writer = act[:, ch : ch + ns]
        reader = act[:, ch + ns :]
        _, step, ld = steps_of(sr, hp[...], heads)
        cum = triangle_sum(lower, ld, heads)
        cum_t = cum.T
        cum_e, step_e = by_channel(cum, step, spread[...])
        last_e = cum_e[q - 1 : q]
        xv = step_e * values
        yield
        scores = dot3(reader, writer, NT)
        yield
        parts = []
        for p in range(ch // 128):
            hi, lo = split(xv[:, 128 * p : 128 * p + 128])
            both = jnp.concatenate([hi, lo], axis=1)
            out = None
            for j in range(128 // size):
                h = p * (128 // size) + j
                decay = jnp.exp(cum[:, h : h + 1] - cum_t[h : h + 1, :])
                ph, plo = split(jnp.where(lower, scores * decay, 0.0))
                r = dot(ph, both)
                one = r[:, :128] + (r[:, 128:] + dot(plo, hi))
                out = one if out is None else jnp.where(lane < j * size, out, one)
                yield
            parts.append(out)
        inner = jnp.concatenate(parts, axis=1)
        old = state[m]
        sin_o[m, 0] = old
        y = inner + jnp.exp(cum_e) * dot3(reader, old, NT) + cp[0:1, :] * values
        decay_ch = jnp.broadcast_to(jnp.exp(last_e), (ns, ch)).T
        state[m] = decay_ch * old + dot3(jnp.exp(last_e - cum_e) * xv, writer, TN)
        yield
        gated = y * (gate * sigmoid(gate))
        outcome = dot(bg_o[m], co[...], NT)
        ones = jnp.ones((8, ch), BF16)
        s1 = dot2(ones, gated * gated, NT)
        s2 = dot2(ones, outcome * cp[1:2, :] * gated, NT)
        row = lax.broadcasted_iota(jnp.int32, s1.shape, 0)
        both_sums = jnp.where(row == 0, s1, jnp.where(row == 1, s2, 0.0))
        for r in range(reps):
            sums_o[r, m] = both_sums
        gate_o[m] = gate
        sig_o[m] = signal[:, :ch]
        pre_o[m] = pre
        y_o[m] = y
        oc_o[m] = outcome
        sr_o[m] = sr
        aside[m] = (pre[:, ch:], signal[:, ch:])
        yield

    side_by_side([work(m) for m in range(micro)])
    for r in range(reps):

        @pl.when(rep == r)
        def _():
            for m in range(micro):
                for out, value in zip((pwr_o, swr_o), aside[m]):
                    beside(out, block % 2, value[:, r * wr : r * wr + wr], m)


def gate_kernel(
    width, ys, gate_r, y_r, oc_r, sums, bg, nrm, cp, send_o, early_o, dy_o, acc_o, cg
):
    q, ch = gate_r.shape
    dp = early_o.shape[0]
    rows = nrm.shape[1] // dp
    piece = (early_o.shape[1] - rows) // 2

    @pl.when(pl.program_id(0) == 0)
    def _():
        cg[...] = jnp.zeros_like(cg)
        early_o[...] = jnp.zeros_like(early_o)
        acc_o[...] = jnp.zeros_like(acc_o)

    s = jnp.sum(sums[:, 0], axis=0)
    scale_row = lax.rsqrt(s[0:1] * (1.0 / width) + EPS)
    mean_row = scale_row * s[1:2] * (1.0 / width)

    def column(v):
        c = jnp.broadcast_to(v, (128, q)).T
        return jnp.concatenate([c] * (ch // 128), axis=1)

    scale = column(scale_row)
    mean = column(mean_row)
    gate = gate_r[...]
    y = y_r[...]
    outcome = oc_r[...]
    gain = cp[1:2, :]
    sg = sigmoid(gate)
    sl = gate * sg
    unit = y * sl * scale
    nout = (unit * gain).astype(BF16)
    cg[...] += dot(nout, bg[...], TN)
    gated_grad = scale * (outcome * gain - unit * mean)
    dy_o[...] = gated_grad * sl
    gg = (gated_grad * y * sg * (1.0 + gate * (1.0 - sg))).astype(BF16)
    early_o[:, :rows, :] += dot(nrm[...], gg, TN).reshape(dp, rows, ch)
    send_o[0, :, :ch] = nout
    send_o[0, :, ch:] = gg
    gain_part = jnp.sum(outcome * unit, axis=0, keepdims=True)
    row = lax.broadcasted_iota(jnp.int32, acc_o.shape, 0)
    acc_o[...] += jnp.where(row == 0, gain_part, 0.0)

    @pl.when(pl.program_id(0) == pl.num_programs(0) - 1)
    def _():
        half = bg.shape[1] // 2
        for d in range(dp):
            start = (d % (dp // ys)) * ys * piece + (d // (dp // ys)) * piece
            part = cg[start : start + piece, :]
            early_o[d, rows : rows + piece, :] = part[:, :half]
            early_o[d, rows + piece :, :] = part[:, half:]


def backward_kernel(
    heads, reps, sig_r, pre_r, y_r, dy_r, sr_r, sin_r, fp, hp, cp, spread, oh,
    vg_o, send_o, wr_o, raw_o, acc_o, hacc_o,
    adj, head_rows,
):
    micro, q, ch = y_r.shape
    cw = fp.shape[1]
    ns = (cw - ch) // 2
    wr = 2 * ns // reps
    size = ch // heads
    block = reps - 1 - pl.program_id(0)

    @pl.when(pl.program_id(0) == 0)
    def _():
        adj[...] = jnp.zeros_like(adj)
        head_rows[...] = jnp.zeros_like(head_rows)
        acc_o[...] = jnp.zeros_like(acc_o)
        hacc_o[...] = jnp.zeros_like(hacc_o)

    lane = lax.broadcasted_iota(jnp.int32, (q, 128), 1)
    lower = triangle(q, True)
    upper = triangle(q, False)
    found = [None] * micro

    def work(m):
        pre = pre_r[m]
        sgm = sigmoid(pre)
        act = pre * sgm
        values = act[:, :ch]
        writer = act[:, ch : ch + ns]
        reader = act[:, ch + ns :]
        moved_raw, step, ld = steps_of(sr_r[m], hp[...], heads)
        cum = triangle_sum(lower, ld, heads)
        cum_t = cum.T
        cum_e, step_e = by_channel(cum, step, spread[...])
        last_e = cum_e[q - 1 : q]
        skip = cp[0:1, :]
        dy = dy_r[m]
        y = y_r[m]
        xv = step_e * values
        yield
        scores = dot3(writer, reader, NT)
        yield
        dscores = jnp.zeros((q, q), F32)
        parts = []
        for p in range(ch // 128):
            dpair = dy[:, 128 * p : 128 * p + 128]
            xpair = xv[:, 128 * p : 128 * p + 128]
            dh, dl = split(dpair)
            dboth = jnp.concatenate([dh, dl], axis=1)
            dtwice = jnp.concatenate([dh, dh], axis=1)
            out = None
            for j in range(128 // size):
                h = p * (128 // size) + j
                decay = jnp.where(upper, jnp.exp(cum_t[h : h + 1, :] - cum[:, h : h + 1]), 0.0)
                ph, plo = split(scores * decay)
                r = dot(ph, dboth)
                one = r[:, :128] + (r[:, 128:] + dot(plo, dh))
                out = one if out is None else jnp.where(lane < j * size, out, one)
                mine = (lane >= j * size) & (lane < (j + 1) * size)
                xh, xl = split(jnp.where(mine, xpair, 0.0))
                got = dot(jnp.concatenate([xh, xl], axis=1), dtwice, NT) + dot(xh, dl, NT)
                dscores = dscores + got * decay
                yield
            parts.append(out)
        inner = jnp.concatenate(parts, axis=1)
        old = adj[m]
        sin = sin_r[m, 0]
        ends = jnp.exp(last_e - cum_e)
        from_state = ends * dot3(writer, old, NT)
        dxv = inner + from_state
        cdy = jnp.exp(cum_e) * dy
        dwriter = dot3(dscores, reader) + dot3(ends * xv, old)
        dreader = dot3(dscores, writer, TN) + dot3(cdy, sin)
        decay_ch = jnp.broadcast_to(jnp.exp(last_e), (ns, ch)).T
        state_row = dot2(jnp.ones((8, ns), BF16), decay_ch * old * sin, NT)[0:1]
        last_row = state_row + jnp.sum(xv * from_state, axis=0, keepdims=True)
        adj[m] = decay_ch * old + dot3(cdy, reader, TN)

        yield
        dstep = dot2(values * dxv, oh[...], NT)
        row = lax.broadcasted_iota(jnp.int32, (q, ch), 0)
        dcum_ch = dy * (y - skip * values) - xv * dxv + jnp.where(row == q - 1, last_row, 0.0)
        dcum = dot2(dcum_ch, oh[...], NT)
        dld = triangle_sum(upper, dcum, heads)
        raw = (dstep - dld * hp[1:2]) * sigmoid(moved_raw)
        raw = jnp.where(lane < heads, raw, 0.0)
        raw_o[m] = jnp.concatenate([jnp.zeros((q, wr), F32), raw[:, : 128 - wr]], axis=1)
        hrow = lax.broadcasted_iota(jnp.int32, hacc_o.shape, 0)
        hacc_o[...] += jnp.where(
            hrow == 0,
            jnp.sum(raw, axis=0, keepdims=True),
            jnp.where(hrow == 1, jnp.sum(dld * ld, axis=0, keepdims=True), 0.0),
        )
        found[m] = jnp.concatenate([dwriter, dreader], axis=1)
        yield

        sv = sgm[:, :ch]
        dpre = (step_e * dxv + skip * dy) * (sv * (1.0 + pre[:, :ch] * (1.0 - sv)))
        ext = jnp.concatenate([dpre, head_rows[m]], axis=0)
        head_rows[m] = dpre[:8]
        signal = sig_r[m]
        total = jnp.zeros_like(dpre)
        rows = []
        for k in range(4):
            moved = ext[3 - k : 3 - k + q]
            total = total + fp[k : k + 1, :ch] * moved
            rows.append(jnp.sum(moved * signal, axis=0, keepdims=True))
        vg = total.astype(BF16)
        vg_o[m] = vg
        send_o[0, :, m * ch : (m + 1) * ch] = vg
        rows.append(jnp.sum(dpre, axis=0, keepdims=True))
        rows.append(jnp.sum(values * dy, axis=0, keepdims=True))
        rows.append(jnp.zeros((2, ch), F32))
        acc_o[...] += jnp.concatenate(rows, axis=0)
        yield

    side_by_side([work(m) for m in range(micro)])
    for m in range(micro):
        for r in range(reps):
            beside(wr_o, block % 2, found[m][:, r * wr : r * wr + wr], r, m)


def tail_kernel(wr, got, pwr, swr, fw, raw, tail_o, send_o, acc_o):
    half = got.shape[1] // 2

    def line(v):
        return jnp.concatenate(
            [v[:half, :wr], v[:half, wr:], v[half:, :wr], v[half:, wr:]], axis=0
        )

    pre = pwr[...]
    s = sigmoid(pre)
    grads = jnp.sum(got[...], axis=0)
    dpre = line(grads * (s * (1.0 + pre * (1.0 - s))))
    signal = line(swr[...])
    total = jnp.zeros_like(dpre)
    ext = jnp.concatenate([dpre, jnp.zeros((8, wr), F32)], axis=0)
    rows = []
    n = dpre.shape[0]
    for k in range(4):
        moved = ext[3 - k : 3 - k + n]
        total = total + fw[k : k + 1, :] * moved
        rows.append(jnp.sum(moved * signal, axis=0, keepdims=True))
    rows.append(jnp.sum(dpre, axis=0, keepdims=True))
    rows.append(jnp.zeros((3, wr), F32))

    @pl.when(pl.program_id(0) == 0)
    def _():
        acc_o[...] = jnp.zeros_like(acc_o)

    acc_o[...] += jnp.concatenate(rows, axis=0)
    wide = jnp.concatenate([total, jnp.zeros((n, 128 - wr), F32)], axis=1)
    tail = (wide + raw[...]).astype(BF16)
    tail_o[...] = tail
    send_o[...] = tail.reshape(send_o.shape)


def mix_kernel(parts, front, perm, mask, residual, out):
    micro, q, width = residual.shape
    ch = perm.shape[0]
    totals = [0.0] * micro
    for k in range(parts.shape[0]):
        rows = contract_rows(front, k, ch, width)
        for m in range(micro):
            moved = dot(parts[k, :, 2 * m * ch : (2 * m + 1) * ch], perm[...]).astype(BF16)
            totals[m] = totals[m] + dot(moved, rows)
    for m in range(micro):
        out[m] = residual[m] + mask[m] * totals[m]


def first_kernel(parts, expand, out):
    micro = out.shape[0]
    reps = parts.shape[0]
    span = expand.shape[1] // reps
    ch = (span - 128) // 2
    totals = [0.0] * micro
    for k in range(reps):
        cols = expand[:, k * span : k * span + ch]
        for m in range(micro):
            totals[m] = totals[m] + dot(parts[k, :, (2 * m + 1) * ch : (2 * m + 2) * ch], cols, NT)
    for m in range(micro):
        out[m] = totals[m]


def last_kernel(part, parts, expand, residual, cotangent, gain, out, norm_o):
    micro, q, width = residual.shape
    reps = parts.shape[0]
    span = expand.shape[1] // reps
    ch = (span - 128) // 2
    totals = [part[m] for m in range(micro)]
    for k in range(reps):
        cols = expand[:, k * span + ch : (k + 1) * span]
        for m in range(micro):
            at = micro * ch + m * 128
            pg = jnp.concatenate([parts[k, :, m * ch : (m + 1) * ch], parts[k, :, at : at + 128]], axis=1)
            totals[m] = totals[m] + dot(pg, cols, NT)
    norm = jnp.zeros((1, width), F32)
    for m in range(micro):
        source = residual[m]
        scale = lax.rsqrt(jnp.mean(source * source, axis=-1, keepdims=True) + EPS)
        unit = source * scale
        norm = norm + jnp.sum(totals[m] * unit, axis=0, keepdims=True)
        scaled = totals[m] * gain[0:1]
        out[m] = cotangent[m] + scale * (
            scaled - unit * jnp.mean(scaled * unit, axis=-1, keepdims=True)
        )
    norm_o[...] = jnp.broadcast_to(norm, norm_o.shape)


def whole(shape):
    return pl.BlockSpec(shape, lambda *b: (0,) * len(shape))


def rows_of(q, width, order=lambda b: b):
    return pl.BlockSpec((q, width), lambda b: (order(b), 0))


SCALAR = pl.BlockSpec(memory_space=pltpu.SMEM)


def params(flops, nbytes, grid=True):
    kinds = dict(dimension_semantics=("arbitrary",)) if grid else {}
    return dict(
        compiler_params=pltpu.CompilerParams(vmem_limit_bytes=VMEM_LIMIT, **kinds),
        cost_estimate=pl.CostEstimate(flops=flops, bytes_accessed=nbytes, transcendentals=0),
    )


def body(
    dims,
    residual, lengths, norm_gain, expand, filters, offsets, gate_gain, contract,
    step_bias, decay_log, skip_gain, cotangent,
):
    ax = Axes(dims)
    micro, _, q, width = residual.shape
    heads_all = step_bias.shape[0]
    reps = lax.axis_size("rep")
    heads = heads_all // reps
    dp = lax.axis_size("dp")
    inner = contract.shape[0] * dp
    ch = inner // reps
    conv = filters.shape[0] * dp
    ns = (conv - inner) // 2
    cw = ch + 2 * ns
    size = inner // heads_all
    total = q * reps
    rep = lax.axis_index("rep")
    rows = expand.shape[0]
    wr = 2 * ns // reps
    sds = jax.ShapeDtypeStruct
    residual = residual[:, 0]
    cotangent = cotangent[:, 0]
    place = rep.astype(jnp.int32).reshape(1)

    def own(a, start, count, dim=-1):
        return lax.dynamic_slice_in_dim(a, start + rep * count, count, a.ndim + dim)

    position = rep * q + jnp.arange(q, dtype=jnp.int32)
    mask = (position[None, :] < lengths[:, :1]).astype(F32)[..., None]
    branch_grad = (mask * cotangent).astype(BF16)

    branch_grad, expand, contract = lax.optimization_barrier((branch_grad, expand, contract))

    half = contract.shape[0] // 2
    front = jnp.concatenate(
        [
            own(expand, 0, ch),
            own(expand, inner, ch),
            expand[:, 2 * inner : 2 * inner + 2 * ns],
            jnp.pad(own(expand, 2 * inner + 2 * ns, heads), ((0, 0), (0, 128 - heads))),
            contract[:half],
            contract[half:],
        ],
        axis=1,
    )
    w_width = ch + cw + 128
    with jax.named_scope("gather_own_expand"):
        front = lax.all_gather(front, "dp", axis=0, tiled=True)
    order = np.arange(ch).reshape(-1, 2, half).transpose(1, 0, 2).reshape(-1)
    perm = np.zeros((ch, ch), np.float32)
    perm[order, np.arange(ch)] = 1.0
    perm = jnp.asarray(perm, BF16)
    small = jnp.concatenate([norm_gain, filters.reshape(-1), offsets, gate_gain])
    sizes = np.cumsum([0, norm_gain.shape[0], filters.size, offsets.shape[0], gate_gain.shape[0]])
    padded = -(-small.shape[0] // 128) * 128
    small = jnp.pad(small, (0, padded - small.shape[0])).reshape(-1, 128)
    with jax.named_scope("gather_small"):
        small, branch_grad = lax.optimization_barrier((small, branch_grad))
        small = jnp.broadcast_to(small[None], (dp,) + small.shape)
        small = lax.all_to_all(small, "dp", 0, 0, tiled=True).reshape(dp, padded).astype(F32)
    with jax.named_scope("gather_branch_grad"):
        bg_near = ax.near_ring(branch_grad)
    gain_one = small[:, sizes[0] : sizes[1]].reshape(1, width)
    filters_full = small[:, sizes[1] : sizes[2]].reshape(conv, 4).T
    offsets_full = small[:, sizes[2] : sizes[3]].reshape(1, conv)
    gain_two = small[:, sizes[3] : sizes[4]].reshape(1, inner)

    scale_one = lax.rsqrt(jnp.mean(residual * residual, axis=-1, keepdims=True) + EPS)
    normed = (residual * scale_one * gain_one).astype(BF16)
    normed, expand, bg_near = lax.optimization_barrier((normed, expand, bg_near))
    with jax.named_scope("gather_normed"):
        nrm_ring = ax.far_ring(normed, *ax.near_ring(normed))
    with jax.named_scope("gather_branch_grad"):
        bg_ring = ax.far_ring(branch_grad, *bg_near)
    expand_cols = jnp.concatenate(
        [
            expand[:, :inner].reshape(rows, reps, ch),
            expand[:, inner : 2 * inner].reshape(rows, reps, ch),
            expand[:, 2 * inner : 2 * inner + 2 * ns].reshape(rows, reps, wr),
            expand[:, 2 * inner + 2 * ns :].reshape(rows, reps, heads),
            jnp.zeros((rows, reps, 128 - wr - heads), BF16),
        ],
        axis=2,
    ).reshape(rows, reps * (2 * ch + 128))
    with jax.named_scope("gather_expand"):
        expand_full = lax.all_gather(expand_cols, "dp", axis=0, tiled=True)

    own_filters = jnp.concatenate(
        [own(filters_full[:, :inner], 0, ch), filters_full[:, inner:]], axis=1
    )
    own_offsets = jnp.concatenate(
        [own(offsets_full[:, :inner], 0, ch), offsets_full[:, inner:]], axis=1
    )
    fp = jnp.concatenate([own_filters, own_offsets, jnp.zeros((3, cw), F32)], axis=0)
    own_skip = own(skip_gain, 0, heads)
    cp = jnp.concatenate(
        [jnp.repeat(own_skip, size)[None], own(gain_two, 0, ch), jnp.zeros((6, ch), F32)], axis=0
    )
    rate = jnp.exp(own(decay_log, 0, heads))
    hp = jnp.pad(jnp.stack([own(step_bias, 0, heads), rate]), ((0, 6), (0, 128 - heads)))
    onehot = np.zeros((128, ch), np.float32)
    onehot[np.arange(ch) // size, np.arange(ch)] = 1.0
    spread_of = np.zeros((128, 2 * ch), np.float32)
    for piece in range(5):
        spread_of[piece * SLOT : (piece + 1) * SLOT, (piece // 3) * ch : (piece // 3 + 1) * ch] = onehot[:SLOT]
    onehot = jnp.asarray(onehot, BF16)
    spread_of = jnp.asarray(spread_of, BF16)

    pieces = whole((micro, q, width))
    ring_specs = [pieces, pieces, pieces, whole((1, q, width)), whole((1, q, width))]
    both = micro * total

    def pairs_of(w, order=lambda b: b):
        return pl.BlockSpec((micro, q, w), lambda b: (0, order(b), 0))

    def pairs(w, dtype=F32):
        return sds((micro, total, w), dtype)

    aside = pl.BlockSpec((micro, q, 2 * wr), lambda b: (0, b // 2, 0))
    kept = pl.pallas_call(
        functools.partial(forward_kernel, heads, reps),
        grid=(reps,),
        in_specs=[SCALAR] + ring_specs * 2 + [
            whole(front.shape), whole((ch, ch)),
            whole((8, cw)), whole((8, 128)), whole((8, ch)), whole((128, 2 * ch)),
        ],
        out_specs=[
            pairs_of(width), pairs_of(width),
            pairs_of(ch), pairs_of(ch), pairs_of(cw), pairs_of(ch), pairs_of(ch), pairs_of(128),
            pl.BlockSpec((micro, 1, ch, ns), lambda b: (0, b, 0, 0)),
            pl.BlockSpec((reps, micro, 8, q), lambda b: (0, 0, 0, b)), aside, aside,
        ],
        out_shape=[
            pairs(width, BF16), pairs(width, BF16),
            pairs(ch), pairs(ch), pairs(cw), pairs(ch), pairs(ch), pairs(128),
            sds((micro, reps, ch, ns), F32), sds((reps, micro, 8, total), F32),
            sds((micro, total // 2, 2 * wr), F32), sds((micro, total // 2, 2 * wr), F32),
        ],
        scratch_shapes=[
            pltpu.VMEM((micro, ch, ns), F32), pltpu.VMEM((micro, 8, cw), F32),
            pltpu.VMEM((ch, width), BF16),
        ],
        name="scan_forward",
        **params(40_000_000_000, 40_000_000),
    )(place, *nrm_ring, *bg_ring, front, perm, fp, hp, cp, spread_of)
    nrm, bg, gate, signal, pre, y, outcome, sr, sin, sums, pwr, swr = kept
    nrm, bg, gate, outcome = (v.reshape(both, -1) for v in (nrm, bg, gate, outcome))
    pwr, swr = (v.reshape(both // 2, -1) for v in (pwr, swr))
    with jax.named_scope("sum_norm_terms"):
        sums, expand_full = lax.optimization_barrier((ax.exchange(sums), expand_full))

    strip = pl.BlockSpec((reps, 1, 8, q), lambda b: (0, b // reps, 0, b % reps))
    ys = ax.size["y"]
    wide = width // 2
    early_rows = rows + 2 * (contract.shape[0] // ys)
    send, early, dy, gain_part = pl.pallas_call(
        functools.partial(gate_kernel, inner, ys),
        grid=(micro * reps,),
        in_specs=[rows_of(q, ch)] * 3 + [strip] + [rows_of(q, width)] * 2 + [whole((8, ch))],
        out_specs=[
            pl.BlockSpec((1, q, 2 * ch), lambda b: (b % reps, 0, b // reps)),
            whole((dp, early_rows, ch)), rows_of(q, ch), whole((8, ch)),
        ],
        out_shape=[
            sds((reps, q, micro * 2 * ch), BF16), sds((dp, early_rows, ch), F32),
            sds((both, ch), F32), sds((8, ch), F32),
        ],
        scratch_shapes=[pltpu.VMEM((ch, width), F32)],
        name="gate_backward",
        **params(8_000_000_000, 20_000_000),
    )(gate, y.reshape(both, ch), outcome, sums, bg, nrm, cp)
    with jax.named_scope("early_sums"):
        early = lax.psum_scatter(early, "dp", scatter_dimension=0)

    with jax.named_scope("send_gate_parts"):
        a_parts = ax.exchange(send)
    def back(b):
        return reps - 1 - b

    value_grads, v_send, wrg, raws, channel_part, head_part = pl.pallas_call(
        functools.partial(backward_kernel, heads, reps),
        grid=(reps,),
        in_specs=[
            pairs_of(ch, back), pairs_of(cw, back), pairs_of(ch, back), pairs_of(ch, back),
            pairs_of(128, back), pl.BlockSpec((micro, 1, ch, ns), lambda b: (0, back(b), 0, 0)),
            whole((8, cw)), whole((8, 128)), whole((8, ch)), whole((128, 2 * ch)), whole((128, ch)),
        ],
        out_specs=[
            pairs_of(ch, back),
            pl.BlockSpec((1, q, micro * ch), lambda b: (back(b), 0, 0)),
            pl.BlockSpec((reps, micro, q, 2 * wr), lambda b: (0, 0, back(b) // 2, 0)),
            pairs_of(128, back), whole((8, ch)), whole((8, 128)),
        ],
        out_shape=[
            pairs(ch, BF16), sds((reps, q, micro * ch), BF16),
            sds((reps, micro, total // 2, 2 * wr), F32),
            pairs(128), sds((8, ch), F32), sds((8, 128), F32),
        ],
        scratch_shapes=[pltpu.VMEM((micro, ch, ns), F32), pltpu.VMEM((micro, 8, ch), F32)],
        name="scan_backward",
        **params(80_000_000_000, 40_000_000),
    )(signal, pre, y, dy.reshape(micro, total, ch), sr, sin, fp, hp, cp, spread_of, onehot)
    value_grads, raws = value_grads.reshape(both, ch), raws.reshape(both, 128)
    wrg = wrg.reshape(reps, both // 2, 2 * wr)
    with jax.named_scope("sum_writer_reader_grad"):
        a_parts, wrg = lax.optimization_barrier((a_parts, wrg))
        wr_got = ax.exchange(wrg)
    vmem = pl.BlockSpec(memory_space=pltpu.VMEM)
    mixed = pl.pallas_call(
        mix_kernel,
        in_specs=[vmem] * 5,
        out_specs=vmem,
        out_shape=sds(residual.shape, F32),
        name="mixed",
        **params(1_200_000_000, 8_000_000, False),
    )(a_parts, front, perm, mask, residual)
    first = pl.pallas_call(
        first_kernel,
        in_specs=[vmem] * 2,
        out_specs=vmem,
        out_shape=sds(residual.shape, F32),
        name="normed_grad_gate",
        **params(1_200_000_000, 8_000_000, False),
    )(a_parts, expand_full)
    with jax.named_scope("late_sums"):
        eg_values = lax.dot_general(nrm, value_grads, TN, preferred_element_type=F32)
    first, mixed, eg_values, wr_got = lax.optimization_barrier((first, mixed, eg_values, wr_got))
    fw = jnp.pad(own(filters_full[:, inner:], 0, wr), ((0, 4), (0, 0)))
    strip = pl.BlockSpec((total // 2, 2 * wr), lambda m: (m, 0))
    tails, t_send, wr_part = pl.pallas_call(
        functools.partial(tail_kernel, wr),
        grid=(micro,),
        in_specs=[
            pl.BlockSpec((reps, total // 2, 2 * wr), lambda m: (0, m, 0)), strip, strip,
            whole((8, wr)), rows_of(total, 128),
        ],
        out_specs=[
            rows_of(total, 128), pl.BlockSpec((reps, q, 128), lambda m: (0, 0, m)), whole((8, wr)),
        ],
        out_shape=[
            sds((both, 128), BF16), sds((reps, q, micro * 128), BF16), sds((8, wr), F32),
        ],
        name="writer_reader_grad",
        **params(100_000_000, 6_000_000),
    )(wr_got, pwr, swr, fw, raws)
    with jax.named_scope("send_values"):
        v_parts = ax.exchange(jnp.concatenate([v_send, t_send], axis=2))

    def spread(a, whole_width):
        blank = jnp.zeros((a.shape[0], whole_width), F32)
        return lax.dynamic_update_slice_in_dim(blank, a, rep * a.shape[1], 1)

    with jax.named_scope("late_sums"):
        taps = jnp.concatenate([spread(channel_part[:5], inner), spread(wr_part[:5], 2 * ns)], axis=1)
        own_heads = jnp.stack(
            [
                head_part[0, :heads],
                head_part[1, :heads],
                jnp.sum(channel_part[5].reshape(heads, size), axis=1),
            ]
        )
        heads_part = jnp.broadcast_to(spread(own_heads, heads_all).reshape(1, -1), (dp, 3 * heads_all))
        per = conv // dp
        flat = jnp.concatenate(
            [
                jnp.transpose(taps.reshape(5, dp, per), (1, 0, 2)).reshape(dp, 5 * per),
                spread(gain_part[:1], inner).reshape(dp, -1),
                heads_part,
            ],
            axis=1,
        )
        cuts = np.cumsum([0, 5 * per, inner // dp, 3 * heads_all])
        block = ch + 128
        spare = 56
        flat = jnp.pad(flat, ((0, 0), (0, rows * spare - flat.shape[1]))).reshape(dp, rows, spare)
        flat = jnp.pad(flat, ((0, 0), (0, 0), (128 - spare, 0)))
        eg_tail = lax.dot_general(nrm, tails, TN, preferred_element_type=F32)
        early, eg_tail = lax.optimization_barrier((early, eg_tail))
        late = jnp.concatenate(
            [eg_values.reshape(dp, rows, ch), eg_tail.reshape(dp, rows, 128) + flat], axis=2
        )
        late = late.reshape(dims + late.shape[1:])
        late = ax.scatter_sum(late, "core", 2)
        late = ax.scatter_sum(late, "x", 1)
        late = ax.scatter_sum(late, "y", 0)
    with jax.named_scope("last_gather"):
        late, v_parts = lax.optimization_barrier((late, v_parts))
        eg_gate = early[:rows]
        cgs = early[rows:]
        if ys == reps:
            turn = [(a * (dp // ys) + e) * reps + b for a in range(ys) for e in range(dp // ys) for b in range(reps)]
            to = [(b * (dp // ys) + e) * reps + a for a in range(ys) for e in range(dp // ys) for b in range(reps)]
            cgs = lax.ppermute(cgs, ("dp", "rep"), list(zip(turn, to)))
        packed = jnp.concatenate([eg_gate.reshape(-1, 128), cgs.reshape(-1, 128), late.reshape(-1, 128)], axis=0)
    residual_grad, norm_part = pl.pallas_call(
        last_kernel,
        in_specs=[vmem] * 6,
        out_specs=[vmem] * 2,
        out_shape=[sds(residual.shape, F32), sds((8, width), F32)],
        name="residual_grad",
        **params(2_000_000_000, 15_000_000, False),
    )(first, v_parts, expand_full, residual, cotangent, gain_one)
    with jax.named_scope("sum_norm_grad"):
        spread_norm = norm_part[:1].reshape(dp, 1, -1)
        spread_norm = jnp.pad(spread_norm, ((0, 0), (0, 0), (0, -spread_norm.shape[2] % 128)))
        norm_sum = jnp.sum(lax.all_to_all(spread_norm, "dp", 0, 0, tiled=True), axis=0)
        norm_sum = jnp.pad(norm_sum.reshape(-1, 128), ((0, -norm_sum.size // 128 % 8), (0, 0)))
    with jax.named_scope("last_gather"):
        got = ax.everywhere(jnp.concatenate([packed, norm_sum], axis=0))
    mark = rows * ch // 128
    eg_gate = got[:, :mark].reshape(reps, rows, ch)
    cgs = got[:, mark : 2 * mark].reshape(reps, 2, -1, wide)
    late = got[:, 2 * mark : packed.shape[0]].reshape(reps, rows, block)
    norm_grad = jnp.sum(got[:, packed.shape[0] :], axis=0).reshape(-1)[: width // dp]
    contract_grad = jnp.concatenate([cgs[:, 0], cgs[:, 1]], axis=2).reshape(-1, width)
    expand_grad = jnp.concatenate(
        [eg_gate[s] for s in range(reps)]
        + [late[s, :rows, :ch] for s in range(reps)]
        + [late[s, :rows, ch : ch + wr] for s in range(reps)]
        + [late[s, :rows, ch + wr : ch + wr + heads] for s in range(reps)],
        axis=1,
    )
    flat = jnp.sum(late[:, :, block - spare :], axis=0).reshape(-1)
    own_taps = flat[: cuts[1]].reshape(5, per)
    gain_grad = flat[cuts[1] : cuts[2]]
    by_head = flat[cuts[2] : cuts[3]].reshape(3, heads_all)
    return (
        mixed[:, None],
        residual_grad[:, None],
        norm_grad,
        expand_grad,
        own_taps[:4].T,
        own_taps[4],
        gain_grad,
        contract_grad,
        by_head[0],
        by_head[1],
        by_head[2],
    )


def solution(mesh):
    dp, rep = mesh.devices.shape
    core = 2 if dp % 8 == 0 else 1
    dims = (rep, dp // (core * rep), core)
    rows = P(None, "dp", "rep", None)
    in_specs = (
        rows, P(None, "dp"), P("dp"), P("dp", None), P("dp", None), P("dp"), P("dp"), P("dp", None),
        P(), P(), P(), rows,
    )
    out_specs = (
        rows, rows, P("dp"), P("dp", None), P("dp", None), P("dp"), P("dp"), P("dp", None),
        P(), P(), P(),
    )
    return jax.shard_map(
        functools.partial(body, dims), mesh=mesh, in_specs=in_specs, out_specs=out_specs, check_vma=False
    )
```

```python
import functools

import jax
import jax.numpy as jnp
import numpy as np
from jax import lax
from jax.experimental import pallas as pl
from jax.experimental.pallas import tpu as pltpu
from jax.sharding import PartitionSpec as P

EPS = 1e-05
F32 = jnp.float32
BF16 = jnp.bfloat16
NN = (((1,), (0,)), ((), ()))
NT = (((1,), (1,)), ((), ()))
TN = (((0,), (0,)), ((), ()))
VMEM_LIMIT = 56 * 1024 * 1024


class Axes:
    def __init__(self, dims):
        self.size = dict(zip(("y", "x", "core"), dims))
        place = lax.axis_index("dp")
        y, x, core = dims
        self.place = {
            "y": place // (x * core),
            "x": (place // core) % x,
            "core": place % core,
            "rep": lax.axis_index("rep"),
        }
        self.size["rep"] = lax.axis_size("rep")

    def shift(self, v, axis, by):
        n = self.size[axis]
        if axis == "rep":
            return lax.ppermute(v, "rep", [(i, (i + by) % n) for i in range(n)])
        stride = {"core": 1, "x": self.size["core"], "y": self.size["core"] * self.size["x"]}[axis]
        route = []
        for i in range(lax.axis_size("dp")):
            at = (i // stride) % n
            route.append((i, i + ((at + by) % n - at) * stride))
        return lax.ppermute(v, "dp", route)

    def near_ring(self, v):
        return self.shift(v, "rep", 1), self.shift(v, "rep", -1)

    def far_ring(self, v, left, right):
        far = (self.shift(left[:1], "rep", 1), self.shift(right[1:], "rep", -1))
        return [v, right, left, far[0], far[1]]

    def exchange(self, v, axis="rep"):
        n = self.size[axis]
        if n == 1:
            return v
        if axis == "rep":
            return lax.all_to_all(v, "rep", 0, 0, tiled=True)
        stride = {"core": 1, "x": self.size["core"], "y": self.size["core"] * self.size["x"]}[axis]
        starts = [i for i in range(lax.axis_size("dp")) if (i // stride) % n == 0]
        groups = [[i + k * stride for k in range(n)] for i in starts]
        return lax.all_to_all(v, "dp", 0, 0, axis_index_groups=groups, tiled=True)

    def everywhere(self, v, axis="rep"):
        return self.exchange(jnp.broadcast_to(v[None], (self.size[axis],) + v.shape), axis)

    def block(self, v, axis, ahead, dim):
        index = (self.place[axis] + ahead) % self.size[axis]
        return lax.dynamic_index_in_dim(v, index, dim, keepdims=False)

    def scatter_sum(self, v, axis, dim):
        total = self.block(v, axis, 0, dim)
        for k in range(1, self.size[axis]):
            total = total + self.shift(self.block(v, axis, k, dim), axis, k)
        return total


def dot(a, b, dims=NN):
    return lax.dot_general(a, b, dims, preferred_element_type=F32)


def split(a):
    hi = a.astype(BF16)
    return hi, (a - hi.astype(F32)).astype(BF16)


def dot3(a, b, dims=NN):
    ah, al = split(a)
    bh, bl = split(b)
    return dot(ah, bh, dims) + (dot(ah, bl, dims) + dot(al, bh, dims))


def dot2(a, b, dims=NN):
    if a.dtype == BF16:
        bh, bl = split(b)
        return dot(a, bh, dims) + dot(a, bl, dims)
    ah, al = split(a)
    return dot(ah, b, dims) + dot(al, b, dims)


SLOT = 8


def three_pieces(v):
    hi = v.astype(BF16).astype(F32)
    rest = v - hi
    mid = rest.astype(BF16).astype(F32)
    low = (rest - mid).astype(BF16).astype(F32)
    return hi + pltpu.roll(mid, SLOT, 1) + pltpu.roll(low, 2 * SLOT, 1)


def triangle_sum(mask, v, heads):
    r = dot(jnp.where(mask, 1.0, 0.0).astype(BF16), three_pieces(v).astype(BF16))
    n = r.shape[1]
    r = r + (pltpu.roll(r, n - SLOT, 1) + pltpu.roll(r, n - 2 * SLOT, 1))
    lane = lax.broadcasted_iota(jnp.int32, r.shape, 1)
    return jnp.where(lane < heads, r, 0.0)


def by_channel(cum, step, spread):
    sh, sl = split(step)
    packed = three_pieces(cum) + (
        pltpu.roll(sh.astype(F32), 3 * SLOT, 1) + pltpu.roll(sl.astype(F32), 4 * SLOT, 1)
    )
    both = dot(packed.astype(BF16), spread)
    half = both.shape[1] // 2
    return both[:, :half], both[:, half:]


def sigmoid(v):
    return 1.0 / (1.0 + jnp.exp(-v))


def steps_of(sr, hp, heads):
    lane = lax.broadcasted_iota(jnp.int32, sr.shape, 1)
    moved = sr + hp[0:1]
    step = jnp.maximum(moved, 0.0) + jnp.log1p(jnp.exp(-jnp.abs(moved)))
    step = jnp.where(lane < heads, step, 0.0)
    return moved, step, -step * hp[1:2]


def triangle(q, lower):
    row = lax.broadcasted_iota(jnp.int32, (q, q), 0)
    col = lax.broadcasted_iota(jnp.int32, (q, q), 1)
    return (row >= col) if lower else (col >= row)


def contract_rows(front, rep, ch, width):
    start = rep * (ch // 2)
    if not isinstance(rep, int):
        start = pl.multiple_of(start, 16)
    pair = front[pl.ds(start, ch // 2), front.shape[1] - 2 * width :]
    return jnp.concatenate([pair[:, :width], pair[:, width:]], axis=0)


def beside(ref, parity, value, *lead):
    half = value.shape[1]
    for odd in (0, 1):

        @pl.when(parity == odd)
        def _():
            ref[(*lead, slice(None), slice(odd * half, odd * half + half))] = value


def pick(out, source, near0, near1, near3, far0, far1):
    for index, ref in ((0, near0), (1, near1), (3, near3)):

        @pl.when(source == index)
        def _():
            out[...] = ref[...]

    @pl.when(source == 2)
    def _():
        out[0] = far0[0]
        out[1] = far1[0]


def side_by_side(works):
    for _ in zip(*works):
        pass


def forward_kernel(
    heads, reps, place, n0, n1, n3, n2a, n2b, b0, b1, b3, b2a, b2b, front, perm, fp, hp, cp, spread,
    nrm_o, bg_o, gate_o, sig_o, pre_o, y_o, oc_o, sr_o, sin_o, sums_o, pwr_o, swr_o,
    state, tail, co,
):
    micro, q = nrm_o.shape[:2]
    ch = cp.shape[1]
    cw = fp.shape[1]
    ns = (cw - ch) // 2
    wr = 2 * ns // reps
    size = ch // heads
    block = pl.program_id(0)
    rep = place[0]
    source = (block - rep + reps) % reps

    pick(nrm_o, source, n0, n1, n3, n2a, n2b)
    pick(bg_o, source, b0, b1, b3, b2a, b2b)

    @pl.when(block == 0)
    def _():
        co[...] = dot(perm[...], contract_rows(front, rep, ch, nrm_o.shape[2])).astype(BF16)
        state[...] = jnp.zeros_like(state)
        tail[...] = jnp.zeros_like(tail)

    aside = [None] * micro
    lane = lax.broadcasted_iota(jnp.int32, (q, 128), 1)
    lower = triangle(q, True)

    def work(m):
        proj = dot(nrm_o[m], front[:, : ch + cw + 128])
        gate = proj[:, :ch]
        signal = proj[:, ch : ch + cw]
        sr = jnp.where(lane < heads, proj[:, ch + cw : ch + cw + 128], 0.0)
        ext = jnp.concatenate([tail[m], signal], axis=0)
        pre = fp[4:5, :] + jnp.zeros_like(signal)
        for k in range(4):
            pre = pre + fp[k : k + 1, :] * ext[5 + k : 5 + k + q]
        tail[m] = signal[q - 8 :]
        yield
        act = pre * sigmoid(pre)
        values = act[:, :ch]
        writer = act[:, ch : ch + ns]
        reader = act[:, ch + ns :]
        _, step, ld = steps_of(sr, hp[...], heads)
        cum = triangle_sum(lower, ld, heads)
        cum_t = cum.T
        cum_e, step_e = by_channel(cum, step, spread[...])
        last_e = cum_e[q - 1 : q]
        xv = step_e * values
        yield
        scores = dot3(reader, writer, NT)
        yield
        parts = []
        for p in range(ch // 128):
            hi, lo = split(xv[:, 128 * p : 128 * p + 128])
            both = jnp.concatenate([hi, lo], axis=1)
            out = None
            for j in range(128 // size):
                h = p * (128 // size) + j
                decay = jnp.exp(cum[:, h : h + 1] - cum_t[h : h + 1, :])
                ph, plo = split(jnp.where(lower, scores * decay, 0.0))
                r = dot(ph, both)
                one = r[:, :128] + (r[:, 128:] + dot(plo, hi))
                out = one if out is None else jnp.where(lane < j * size, out, one)
                yield
            parts.append(out)
        inner = jnp.concatenate(parts, axis=1)
        old = state[m]
        sin_o[m, 0] = old
        y = inner + jnp.exp(cum_e) * dot3(reader, old, NT) + cp[0:1, :] * values
        decay_ch = jnp.broadcast_to(jnp.exp(last_e), (ns, ch)).T
        state[m] = decay_ch * old + dot3(jnp.exp(last_e - cum_e) * xv, writer, TN)
        yield
        gated = y * (gate * sigmoid(gate))
        outcome = dot(bg_o[m], co[...], NT)
        ones = jnp.ones((8, ch), BF16)
        s1 = dot2(ones, gated * gated, NT)
        s2 = dot2(ones, outcome * cp[1:2, :] * gated, NT)
        for r in range(reps):
            sums_o[r, 2 * m : 2 * m + 2, :] = jnp.concatenate([s1[0:1], s2[0:1]], axis=0)
        gate_o[m] = gate
        sig_o[m] = signal[:, :ch]
        pre_o[m] = pre
        y_o[m] = y
        oc_o[m] = outcome
        sr_o[m] = sr
        aside[m] = (pre[:, ch:], signal[:, ch:])
        yield

    side_by_side([work(m) for m in range(micro)])
    for r in range(reps):

        @pl.when(rep == r)
        def _():
            for m in range(micro):
                for out, value in zip((pwr_o, swr_o), aside[m]):
                    beside(out, block % 2, value[:, r * wr : r * wr + wr], m)


def gate_kernel(
    width, ys, gate_r, y_r, oc_r, sums, bg, nrm, cp, send_o, early_o, dy_o, acc_o, cg
):
    q, ch = gate_r.shape
    dp = early_o.shape[0]
    rows = nrm.shape[1] // dp
    piece = (early_o.shape[1] - rows) // 2

    @pl.when(pl.program_id(0) == 0)
    def _():
        cg[...] = jnp.zeros_like(cg)
        early_o[...] = jnp.zeros_like(early_o)
        acc_o[...] = jnp.zeros_like(acc_o)

    s = jnp.sum(sums[...], axis=0)
    s = jnp.where(pl.program_id(0) < sums.shape[0], s[0:2], s[2:4])
    scale_row = lax.rsqrt(s[0:1] * (1.0 / width) + EPS)
    mean_row = scale_row * s[1:2] * (1.0 / width)

    def column(v):
        c = jnp.broadcast_to(v, (128, q)).T
        return jnp.concatenate([c] * (ch // 128), axis=1)

    scale = column(scale_row)
    mean = column(mean_row)
    gate = gate_r[...]
    y = y_r[...]
    outcome = oc_r[...]
    gain = cp[1:2, :]
    sg = sigmoid(gate)
    sl = gate * sg
    unit = y * sl * scale
    nout = (unit * gain).astype(BF16)
    cg[...] += dot(nout, bg[...], TN)
    gated_grad = scale * (outcome * gain - unit * mean)
    dy_o[...] = gated_grad * sl
    gg = (gated_grad * y * sg * (1.0 + gate * (1.0 - sg))).astype(BF16)
    early_o[:, :rows, :] += dot(nrm[...], gg, TN).reshape(dp, rows, ch)
    send_o[0, :, :ch] = nout
    send_o[0, :, ch:] = gg
    gain_part = jnp.sum(outcome * unit, axis=0, keepdims=True)
    row = lax.broadcasted_iota(jnp.int32, acc_o.shape, 0)
    acc_o[...] += jnp.where(row == 0, gain_part, 0.0)

    @pl.when(pl.program_id(0) == pl.num_programs(0) - 1)
    def _():
        half = bg.shape[1] // 2
        for d in range(dp):
            start = (d % (dp // ys)) * ys * piece + (d // (dp // ys)) * piece
            part = cg[start : start + piece, :]
            early_o[d, rows : rows + piece, :] = part[:, :half]
            early_o[d, rows + piece :, :] = part[:, half:]


def backward_kernel(
    heads, reps, sig_r, pre_r, y_r, dy_r, sr_r, sin_r, fp, hp, cp, spread, oh,
    vg_o, send_o, wr_o, raw_o, acc_o, hacc_o,
    adj, head_rows,
):
    micro, q, ch = y_r.shape
    cw = fp.shape[1]
    ns = (cw - ch) // 2
    wr = 2 * ns // reps
    size = ch // heads
    block = reps - 1 - pl.program_id(0)

    @pl.when(pl.program_id(0) == 0)
    def _():
        adj[...] = jnp.zeros_like(adj)
        head_rows[...] = jnp.zeros_like(head_rows)
        acc_o[...] = jnp.zeros_like(acc_o)
        hacc_o[...] = jnp.zeros_like(hacc_o)

    lane = lax.broadcasted_iota(jnp.int32, (q, 128), 1)
    lower = triangle(q, True)
    upper = triangle(q, False)
    found = [None] * micro

    def work(m):
        pre = pre_r[m]
        sgm = sigmoid(pre)
        act = pre * sgm
        values = act[:, :ch]
        writer = act[:, ch : ch + ns]
        reader = act[:, ch + ns :]
        moved_raw, step, ld = steps_of(sr_r[m], hp[...], heads)
        cum = triangle_sum(lower, ld, heads)
        cum_t = cum.T
        cum_e, step_e = by_channel(cum, step, spread[...])
        last_e = cum_e[q - 1 : q]
        skip = cp[0:1, :]
        dy = dy_r[m]
        y = y_r[m]
        xv = step_e * values
        yield
        scores = dot3(writer, reader, NT)
        yield
        dscores = jnp.zeros((q, q), F32)
        parts = []
        for p in range(ch // 128):
            dpair = dy[:, 128 * p : 128 * p + 128]
            xpair = xv[:, 128 * p : 128 * p + 128]
            dh, dl = split(dpair)
            dboth = jnp.concatenate([dh, dl], axis=1)
            dtwice = jnp.concatenate([dh, dh], axis=1)
            out = None
            for j in range(128 // size):
                h = p * (128 // size) + j
                decay = jnp.where(upper, jnp.exp(cum_t[h : h + 1, :] - cum[:, h : h + 1]), 0.0)
                ph, plo = split(scores * decay)
                r = dot(ph, dboth)
                one = r[:, :128] + (r[:, 128:] + dot(plo, dh))
                out = one if out is None else jnp.where(lane < j * size, out, one)
                mine = (lane >= j * size) & (lane < (j + 1) * size)
                xh, xl = split(jnp.where(mine, xpair, 0.0))
                got = dot(jnp.concatenate([xh, xl], axis=1), dtwice, NT) + dot(xh, dl, NT)
                dscores = dscores + got * decay
                yield
            parts.append(out)
        inner = jnp.concatenate(parts, axis=1)
        old = adj[m]
        sin = sin_r[m, 0]
        ends = jnp.exp(last_e - cum_e)
        from_state = ends * dot3(writer, old, NT)
        dxv = inner + from_state
        cdy = jnp.exp(cum_e) * dy
        dwriter = dot3(dscores, reader) + dot3(ends * xv, old)
        dreader = dot3(dscores, writer, TN) + dot3(cdy, sin)
        decay_ch = jnp.broadcast_to(jnp.exp(last_e), (ns, ch)).T
        state_row = dot2(jnp.ones((8, ns), BF16), decay_ch * old * sin, NT)[0:1]
        last_row = state_row + jnp.sum(xv * from_state, axis=0, keepdims=True)
        adj[m] = decay_ch * old + dot3(cdy, reader, TN)

        yield
        dstep = dot2(values * dxv, oh[...], NT)
        row = lax.broadcasted_iota(jnp.int32, (q, ch), 0)
        dcum_ch = dy * (y - skip * values) - xv * dxv + jnp.where(row == q - 1, last_row, 0.0)
        dcum = dot2(dcum_ch, oh[...], NT)
        dld = triangle_sum(upper, dcum, heads)
        raw = (dstep - dld * hp[1:2]) * sigmoid(moved_raw)
        raw = jnp.where(lane < heads, raw, 0.0)
        raw_o[m] = jnp.concatenate([jnp.zeros((q, wr), F32), raw[:, : 128 - wr]], axis=1)
        hrow = lax.broadcasted_iota(jnp.int32, hacc_o.shape, 0)
        hacc_o[...] += jnp.where(
            hrow == 0,
            jnp.sum(raw, axis=0, keepdims=True),
            jnp.where(hrow == 1, jnp.sum(dld * ld, axis=0, keepdims=True), 0.0),
        )
        found[m] = jnp.concatenate([dwriter, dreader], axis=1)
        yield

        sv = sgm[:, :ch]
        dpre = (step_e * dxv + skip * dy) * (sv * (1.0 + pre[:, :ch] * (1.0 - sv)))
        ext = jnp.concatenate([dpre, head_rows[m]], axis=0)
        head_rows[m] = dpre[:8]
        signal = sig_r[m]
        total = jnp.zeros_like(dpre)
        rows = []
        for k in range(4):
            moved = ext[3 - k : 3 - k + q]
            total = total + fp[k : k + 1, :ch] * moved
            rows.append(jnp.sum(moved * signal, axis=0, keepdims=True))
        vg = total.astype(BF16)
        vg_o[m] = vg
        send_o[0, :, m * ch : (m + 1) * ch] = vg
        rows.append(jnp.sum(dpre, axis=0, keepdims=True))
        rows.append(jnp.sum(values * dy, axis=0, keepdims=True))
        rows.append(jnp.zeros((2, ch), F32))
        acc_o[...] += jnp.concatenate(rows, axis=0)
        yield

    side_by_side([work(m) for m in range(micro)])
    for m in range(micro):
        for r in range(reps):
            beside(wr_o, block % 2, found[m][:, r * wr : r * wr + wr], r, m)


def tail_kernel(wr, got, pwr, swr, fw, raw, tail_o, send_o, acc_o):
    half = got.shape[1] // 2

    def line(v):
        return jnp.concatenate(
            [v[:half, :wr], v[:half, wr:], v[half:, :wr], v[half:, wr:]], axis=0
        )

    pre = pwr[...]
    s = sigmoid(pre)
    grads = jnp.sum(got[...], axis=0)
    dpre = line(grads * (s * (1.0 + pre * (1.0 - s))))
    signal = line(swr[...])
    total = jnp.zeros_like(dpre)
    ext = jnp.concatenate([dpre, jnp.zeros((8, wr), F32)], axis=0)
    rows = []
    n = dpre.shape[0]
    for k in range(4):
        moved = ext[3 - k : 3 - k + n]
        total = total + fw[k : k + 1, :] * moved
        rows.append(jnp.sum(moved * signal, axis=0, keepdims=True))
    rows.append(jnp.sum(dpre, axis=0, keepdims=True))
    rows.append(jnp.zeros((3, wr), F32))

    @pl.when(pl.program_id(0) == 0)
    def _():
        acc_o[...] = jnp.zeros_like(acc_o)

    acc_o[...] += jnp.concatenate(rows, axis=0)
    wide = jnp.concatenate([total, jnp.zeros((n, 128 - wr), F32)], axis=1)
    tail = (wide + raw[...]).astype(BF16)
    tail_o[...] = tail
    send_o[...] = tail.reshape(send_o.shape)


def mix_kernel(parts, front, perm, mask, residual, out):
    micro, q, width = residual.shape
    ch = perm.shape[0]
    totals = [0.0] * micro
    for k in range(parts.shape[0]):
        rows = contract_rows(front, k, ch, width)
        for m in range(micro):
            moved = dot(parts[k, :, 2 * m * ch : (2 * m + 1) * ch], perm[...]).astype(BF16)
            totals[m] = totals[m] + dot(moved, rows)
    for m in range(micro):
        out[m] = residual[m] + mask[m] * totals[m]


def first_kernel(parts, expand, out):
    micro = out.shape[0]
    reps = parts.shape[0]
    span = expand.shape[1] // reps
    ch = (span - 128) // 2
    totals = [0.0] * micro
    for k in range(reps):
        cols = expand[:, k * span : k * span + ch]
        for m in range(micro):
            totals[m] = totals[m] + dot(parts[k, :, (2 * m + 1) * ch : (2 * m + 2) * ch], cols, NT)
    for m in range(micro):
        out[m] = totals[m]


def last_kernel(part, parts, expand, residual, cotangent, gain, out, norm_o):
    micro, q, width = residual.shape
    reps = parts.shape[0]
    span = expand.shape[1] // reps
    ch = (span - 128) // 2
    totals = [part[m] for m in range(micro)]
    for k in range(reps):
        cols = expand[:, k * span + ch : (k + 1) * span]
        for m in range(micro):
            at = micro * ch + m * 128
            pg = jnp.concatenate([parts[k, :, m * ch : (m + 1) * ch], parts[k, :, at : at + 128]], axis=1)
            totals[m] = totals[m] + dot(pg, cols, NT)
    norm = jnp.zeros((1, width), F32)
    for m in range(micro):
        source = residual[m]
        scale = lax.rsqrt(jnp.mean(source * source, axis=-1, keepdims=True) + EPS)
        unit = source * scale
        norm = norm + jnp.sum(totals[m] * unit, axis=0, keepdims=True)
        scaled = totals[m] * gain[0:1]
        out[m] = cotangent[m] + scale * (
            scaled - unit * jnp.mean(scaled * unit, axis=-1, keepdims=True)
        )
    norm_o[...] = jnp.broadcast_to(norm, norm_o.shape)


def whole(shape):
    return pl.BlockSpec(shape, lambda *b: (0,) * len(shape))


def rows_of(q, width, order=lambda b: b):
    return pl.BlockSpec((q, width), lambda b: (order(b), 0))


SCALAR = pl.BlockSpec(memory_space=pltpu.SMEM)


def params(flops, nbytes, grid=True):
    kinds = dict(dimension_semantics=("arbitrary",)) if grid else {}
    return dict(
        compiler_params=pltpu.CompilerParams(vmem_limit_bytes=VMEM_LIMIT, **kinds),
        cost_estimate=pl.CostEstimate(flops=flops, bytes_accessed=nbytes, transcendentals=0),
    )


def body(
    dims,
    residual, lengths, norm_gain, expand, filters, offsets, gate_gain, contract,
    step_bias, decay_log, skip_gain, cotangent,
):
    ax = Axes(dims)
    micro, _, q, width = residual.shape
    heads_all = step_bias.shape[0]
    reps = lax.axis_size("rep")
    heads = heads_all // reps
    dp = lax.axis_size("dp")
    inner = contract.shape[0] * dp
    ch = inner // reps
    conv = filters.shape[0] * dp
    ns = (conv - inner) // 2
    cw = ch + 2 * ns
    size = inner // heads_all
    total = q * reps
    rep = lax.axis_index("rep")
    rows = expand.shape[0]
    wr = 2 * ns // reps
    sds = jax.ShapeDtypeStruct
    residual = residual[:, 0]
    cotangent = cotangent[:, 0]
    place = rep.astype(jnp.int32).reshape(1)

    def own(a, start, count, dim=-1):
        return lax.dynamic_slice_in_dim(a, start + rep * count, count, a.ndim + dim)

    position = rep * q + jnp.arange(q, dtype=jnp.int32)
    mask = (position[None, :] < lengths[:, :1]).astype(F32)[..., None]
    branch_grad = (mask * cotangent).astype(BF16)

    branch_grad, expand, contract = lax.optimization_barrier((branch_grad, expand, contract))

    half = contract.shape[0] // 2
    front = jnp.concatenate(
        [
            own(expand, 0, ch),
            own(expand, inner, ch),
            expand[:, 2 * inner : 2 * inner + 2 * ns],
            jnp.pad(own(expand, 2 * inner + 2 * ns, heads), ((0, 0), (0, 128 - heads))),
            contract[:half],
            contract[half:],
        ],
        axis=1,
    )
    w_width = ch + cw + 128
    with jax.named_scope("gather_own_expand"):
        front = lax.all_gather(front, "dp", axis=0, tiled=True)
    order = np.arange(ch).reshape(-1, 2, half).transpose(1, 0, 2).reshape(-1)
    perm = np.zeros((ch, ch), np.float32)
    perm[order, np.arange(ch)] = 1.0
    perm = jnp.asarray(perm, BF16)
    small = jnp.concatenate([norm_gain, filters.reshape(-1), offsets, gate_gain])
    sizes = np.cumsum([0, norm_gain.shape[0], filters.size, offsets.shape[0], gate_gain.shape[0]])
    padded = -(-small.shape[0] // 128) * 128
    small = jnp.pad(small, (0, padded - small.shape[0])).reshape(-1, 128)
    with jax.named_scope("gather_small"):
        small, branch_grad = lax.optimization_barrier((small, branch_grad))
        small = jnp.broadcast_to(small[None], (dp,) + small.shape)
        small = lax.all_to_all(small, "dp", 0, 0, tiled=True).reshape(dp, padded).astype(F32)
    with jax.named_scope("gather_branch_grad"):
        bg_near = ax.near_ring(branch_grad)
    gain_one = small[:, sizes[0] : sizes[1]].reshape(1, width)
    filters_full = small[:, sizes[1] : sizes[2]].reshape(conv, 4).T
    offsets_full = small[:, sizes[2] : sizes[3]].reshape(1, conv)
    gain_two = small[:, sizes[3] : sizes[4]].reshape(1, inner)

    scale_one = lax.rsqrt(jnp.mean(residual * residual, axis=-1, keepdims=True) + EPS)
    normed = (residual * scale_one * gain_one).astype(BF16)
    normed, expand, bg_near = lax.optimization_barrier((normed, expand, bg_near))
    with jax.named_scope("gather_normed"):
        nrm_ring = ax.far_ring(normed, *ax.near_ring(normed))
    with jax.named_scope("gather_branch_grad"):
        bg_ring = ax.far_ring(branch_grad, *bg_near)
    expand_cols = jnp.concatenate(
        [
            expand[:, :inner].reshape(rows, reps, ch),
            expand[:, inner : 2 * inner].reshape(rows, reps, ch),
            expand[:, 2 * inner : 2 * inner + 2 * ns].reshape(rows, reps, wr),
            expand[:, 2 * inner + 2 * ns :].reshape(rows, reps, heads),
            jnp.zeros((rows, reps, 128 - wr - heads), BF16),
        ],
        axis=2,
    ).reshape(rows, reps * (2 * ch + 128))
    with jax.named_scope("gather_expand"):
        expand_full = lax.all_gather(expand_cols, "dp", axis=0, tiled=True)

    own_filters = jnp.concatenate(
        [own(filters_full[:, :inner], 0, ch), filters_full[:, inner:]], axis=1
    )
    own_offsets = jnp.concatenate(
        [own(offsets_full[:, :inner], 0, ch), offsets_full[:, inner:]], axis=1
    )
    fp = jnp.concatenate([own_filters, own_offsets, jnp.zeros((3, cw), F32)], axis=0)
    own_skip = own(skip_gain, 0, heads)
    cp = jnp.concatenate(
        [jnp.repeat(own_skip, size)[None], own(gain_two, 0, ch), jnp.zeros((6, ch), F32)], axis=0
    )
    rate = jnp.exp(own(decay_log, 0, heads))
    hp = jnp.pad(jnp.stack([own(step_bias, 0, heads), rate]), ((0, 6), (0, 128 - heads)))
    onehot = np.zeros((128, ch), np.float32)
    onehot[np.arange(ch) // size, np.arange(ch)] = 1.0
    spread_of = np.zeros((128, 2 * ch), np.float32)
    for piece in range(5):
        spread_of[piece * SLOT : (piece + 1) * SLOT, (piece // 3) * ch : (piece // 3 + 1) * ch] = onehot[:SLOT]
    onehot = jnp.asarray(onehot, BF16)
    spread_of = jnp.asarray(spread_of, BF16)

    pieces = whole((micro, q, width))
    ring_specs = [pieces, pieces, pieces, whole((1, q, width)), whole((1, q, width))]
    both = micro * total

    def pairs_of(w, order=lambda b: b):
        return pl.BlockSpec((micro, q, w), lambda b: (0, order(b), 0))

    def pairs(w, dtype=F32):
        return sds((micro, total, w), dtype)

    aside = pl.BlockSpec((micro, q, 2 * wr), lambda b: (0, b // 2, 0))
    kept = pl.pallas_call(
        functools.partial(forward_kernel, heads, reps),
        grid=(reps,),
        in_specs=[SCALAR] + ring_specs * 2 + [
            whole(front.shape), whole((ch, ch)),
            whole((8, cw)), whole((8, 128)), whole((8, ch)), whole((128, 2 * ch)),
        ],
        out_specs=[
            pairs_of(width), pairs_of(width),
            pairs_of(ch), pairs_of(ch), pairs_of(cw), pairs_of(ch), pairs_of(ch), pairs_of(128),
            pl.BlockSpec((micro, 1, ch, ns), lambda b: (0, b, 0, 0)),
            pl.BlockSpec((reps, 2 * micro, q), lambda b: (0, 0, b)), aside, aside,
        ],
        out_shape=[
            pairs(width, BF16), pairs(width, BF16),
            pairs(ch), pairs(ch), pairs(cw), pairs(ch), pairs(ch), pairs(128),
            sds((micro, reps, ch, ns), F32), sds((reps, 2 * micro, total), F32),
            sds((micro, total // 2, 2 * wr), F32), sds((micro, total // 2, 2 * wr), F32),
        ],
        scratch_shapes=[
            pltpu.VMEM((micro, ch, ns), F32), pltpu.VMEM((micro, 8, cw), F32),
            pltpu.VMEM((ch, width), BF16),
        ],
        name="scan_forward",
        **params(40_000_000_000, 40_000_000),
    )(place, *nrm_ring, *bg_ring, front, perm, fp, hp, cp, spread_of)
    nrm, bg, gate, signal, pre, y, outcome, sr, sin, sums, pwr, swr = kept
    nrm, bg, gate, outcome = (v.reshape(both, -1) for v in (nrm, bg, gate, outcome))
    pwr, swr = (v.reshape(both // 2, -1) for v in (pwr, swr))
    with jax.named_scope("sum_norm_terms"):
        sums, expand_full = lax.optimization_barrier((ax.exchange(sums), expand_full))

    strip = pl.BlockSpec((reps, 2 * micro, q), lambda b: (0, 0, b % reps))
    ys = ax.size["y"]
    wide = width // 2
    early_rows = rows + 2 * (contract.shape[0] // ys)
    send, early, dy, gain_part = pl.pallas_call(
        functools.partial(gate_kernel, inner, ys),
        grid=(micro * reps,),
        in_specs=[rows_of(q, ch)] * 3 + [strip] + [rows_of(q, width)] * 2 + [whole((8, ch))],
        out_specs=[
            pl.BlockSpec((1, q, 2 * ch), lambda b: (b % reps, 0, b // reps)),
            whole((dp, early_rows, ch)), rows_of(q, ch), whole((8, ch)),
        ],
        out_shape=[
            sds((reps, q, micro * 2 * ch), BF16), sds((dp, early_rows, ch), F32),
            sds((both, ch), F32), sds((8, ch), F32),
        ],
        scratch_shapes=[pltpu.VMEM((ch, width), F32)],
        name="gate_backward",
        **params(8_000_000_000, 20_000_000),
    )(gate, y.reshape(both, ch), outcome, sums, bg, nrm, cp)
    with jax.named_scope("early_sums"):
        early = lax.psum_scatter(early, "dp", scatter_dimension=0)

    with jax.named_scope("send_gate_parts"):
        a_parts = ax.exchange(send)
    def back(b):
        return reps - 1 - b

    value_grads, v_send, wrg, raws, channel_part, head_part = pl.pallas_call(
        functools.partial(backward_kernel, heads, reps),
        grid=(reps,),
        in_specs=[
            pairs_of(ch, back), pairs_of(cw, back), pairs_of(ch, back), pairs_of(ch, back),
            pairs_of(128, back), pl.BlockSpec((micro, 1, ch, ns), lambda b: (0, back(b), 0, 0)),
            whole((8, cw)), whole((8, 128)), whole((8, ch)), whole((128, 2 * ch)), whole((128, ch)),
        ],
        out_specs=[
            pairs_of(ch, back),
            pl.BlockSpec((1, q, micro * ch), lambda b: (back(b), 0, 0)),
            pl.BlockSpec((reps, micro, q, 2 * wr), lambda b: (0, 0, back(b) // 2, 0)),
            pairs_of(128, back), whole((8, ch)), whole((8, 128)),
        ],
        out_shape=[
            pairs(ch, BF16), sds((reps, q, micro * ch), BF16),
            sds((reps, micro, total // 2, 2 * wr), F32),
            pairs(128), sds((8, ch), F32), sds((8, 128), F32),
        ],
        scratch_shapes=[pltpu.VMEM((micro, ch, ns), F32), pltpu.VMEM((micro, 8, ch), F32)],
        name="scan_backward",
        **params(80_000_000_000, 40_000_000),
    )(signal, pre, y, dy.reshape(micro, total, ch), sr, sin, fp, hp, cp, spread_of, onehot)
    value_grads, raws = value_grads.reshape(both, ch), raws.reshape(both, 128)
    wrg = wrg.reshape(reps, both // 2, 2 * wr)
    with jax.named_scope("sum_writer_reader_grad"):
        a_parts, wrg = lax.optimization_barrier((a_parts, wrg))
        wr_got = ax.exchange(wrg)
    vmem = pl.BlockSpec(memory_space=pltpu.VMEM)
    mixed = pl.pallas_call(
        mix_kernel,
        in_specs=[vmem] * 5,
        out_specs=vmem,
        out_shape=sds(residual.shape, F32),
        name="mixed",
        **params(1_200_000_000, 8_000_000, False),
    )(a_parts, front, perm, mask, residual)
    first = pl.pallas_call(
        first_kernel,
        in_specs=[vmem] * 2,
        out_specs=vmem,
        out_shape=sds(residual.shape, F32),
        name="normed_grad_gate",
        **params(1_200_000_000, 8_000_000, False),
    )(a_parts, expand_full)
    with jax.named_scope("late_sums"):
        eg_values = lax.dot_general(nrm, value_grads, TN, preferred_element_type=F32)
    first, mixed, eg_values, wr_got = lax.optimization_barrier((first, mixed, eg_values, wr_got))
    fw = jnp.pad(own(filters_full[:, inner:], 0, wr), ((0, 4), (0, 0)))
    strip = pl.BlockSpec((total // 2, 2 * wr), lambda m: (m, 0))
    tails, t_send, wr_part = pl.pallas_call(
        functools.partial(tail_kernel, wr),
        grid=(micro,),
        in_specs=[
            pl.BlockSpec((reps, total // 2, 2 * wr), lambda m: (0, m, 0)), strip, strip,
            whole((8, wr)), rows_of(total, 128),
        ],
        out_specs=[
            rows_of(total, 128), pl.BlockSpec((reps, q, 128), lambda m: (0, 0, m)), whole((8, wr)),
        ],
        out_shape=[
            sds((both, 128), BF16), sds((reps, q, micro * 128), BF16), sds((8, wr), F32),
        ],
        name="writer_reader_grad",
        **params(100_000_000, 6_000_000),
    )(wr_got, pwr, swr, fw, raws)
    with jax.named_scope("send_values"):
        v_parts = ax.exchange(jnp.concatenate([v_send, t_send], axis=2))

    def spread(a, whole_width):
        blank = jnp.zeros((a.shape[0], whole_width), F32)
        return lax.dynamic_update_slice_in_dim(blank, a, rep * a.shape[1], 1)

    with jax.named_scope("late_sums"):
        taps = jnp.concatenate([spread(channel_part[:5], inner), spread(wr_part[:5], 2 * ns)], axis=1)
        own_heads = jnp.stack(
            [
                head_part[0, :heads],
                head_part[1, :heads],
                jnp.sum(channel_part[5].reshape(heads, size), axis=1),
            ]
        )
        heads_part = jnp.broadcast_to(spread(own_heads, heads_all).reshape(1, -1), (dp, 3 * heads_all))
        per = conv // dp
        flat = jnp.concatenate(
            [
                jnp.transpose(taps.reshape(5, dp, per), (1, 0, 2)).reshape(dp, 5 * per),
                spread(gain_part[:1], inner).reshape(dp, -1),
                heads_part,
            ],
            axis=1,
        )
        cuts = np.cumsum([0, 5 * per, inner // dp, 3 * heads_all])
        block = ch + 128
        spare = 56
        flat = jnp.pad(flat, ((0, 0), (0, rows * spare - flat.shape[1]))).reshape(dp, rows, spare)
        flat = jnp.pad(flat, ((0, 0), (0, 0), (128 - spare, 0)))
        eg_tail = lax.dot_general(nrm, tails, TN, preferred_element_type=F32)
        early, eg_tail = lax.optimization_barrier((early, eg_tail))
        late = jnp.concatenate(
            [eg_values.reshape(dp, rows, ch), eg_tail.reshape(dp, rows, 128) + flat], axis=2
        )
        late = late.reshape(dims + late.shape[1:])
        late = ax.scatter_sum(late, "core", 2)
        late = ax.scatter_sum(late, "x", 1)
        late = ax.scatter_sum(late, "y", 0)
    with jax.named_scope("last_gather"):
        late, v_parts = lax.optimization_barrier((late, v_parts))
        eg_gate = early[:rows]
        cgs = early[rows:]
        if ys == reps:
            turn = [(a * (dp // ys) + e) * reps + b for a in range(ys) for e in range(dp // ys) for b in range(reps)]
            to = [(b * (dp // ys) + e) * reps + a for a in range(ys) for e in range(dp // ys) for b in range(reps)]
            cgs = lax.ppermute(cgs, ("dp", "rep"), list(zip(turn, to)))
        packed = jnp.concatenate([eg_gate.reshape(-1, 128), cgs.reshape(-1, 128), late.reshape(-1, 128)], axis=0)
    residual_grad, norm_part = pl.pallas_call(
        last_kernel,
        in_specs=[vmem] * 6,
        out_specs=[vmem] * 2,
        out_shape=[sds(residual.shape, F32), sds((8, width), F32)],
        name="residual_grad",
        **params(2_000_000_000, 15_000_000, False),
    )(first, v_parts, expand_full, residual, cotangent, gain_one)
    with jax.named_scope("sum_norm_grad"):
        spread_norm = norm_part[:1].reshape(dp, 1, -1)
        spread_norm = jnp.pad(spread_norm, ((0, 0), (0, 0), (0, -spread_norm.shape[2] % 128)))
        norm_sum = jnp.sum(lax.all_to_all(spread_norm, "dp", 0, 0, tiled=True), axis=0)
        norm_sum = jnp.pad(norm_sum.reshape(-1, 128), ((0, -norm_sum.size // 128 % 8), (0, 0)))
    with jax.named_scope("last_gather"):
        got = ax.everywhere(jnp.concatenate([packed, norm_sum], axis=0))
    mark = rows * ch // 128
    eg_gate = got[:, :mark].reshape(reps, rows, ch)
    cgs = got[:, mark : 2 * mark].reshape(reps, 2, -1, wide)
    late = got[:, 2 * mark : packed.shape[0]].reshape(reps, rows, block)
    norm_grad = jnp.sum(got[:, packed.shape[0] :], axis=0).reshape(-1)[: width // dp]
    contract_grad = jnp.concatenate([cgs[:, 0], cgs[:, 1]], axis=2).reshape(-1, width)
    expand_grad = jnp.concatenate(
        [eg_gate[s] for s in range(reps)]
        + [late[s, :rows, :ch] for s in range(reps)]
        + [late[s, :rows, ch : ch + wr] for s in range(reps)]
        + [late[s, :rows, ch + wr : ch + wr + heads] for s in range(reps)],
        axis=1,
    )
    flat = jnp.sum(late[:, :, block - spare :], axis=0).reshape(-1)
    own_taps = flat[: cuts[1]].reshape(5, per)
    gain_grad = flat[cuts[1] : cuts[2]]
    by_head = flat[cuts[2] : cuts[3]].reshape(3, heads_all)
    return (
        mixed[:, None],
        residual_grad[:, None],
        norm_grad,
        expand_grad,
        own_taps[:4].T,
        own_taps[4],
        gain_grad,
        contract_grad,
        by_head[0],
        by_head[1],
        by_head[2],
    )


def solution(mesh):
    dp, rep = mesh.devices.shape
    core = 2 if dp % 8 == 0 else 1
    dims = (rep, dp // (core * rep), core)
    rows = P(None, "dp", "rep", None)
    in_specs = (
        rows, P(None, "dp"), P("dp"), P("dp", None), P("dp", None), P("dp"), P("dp"), P("dp", None),
        P(), P(), P(), rows,
    )
    out_specs = (
        rows, rows, P("dp"), P("dp", None), P("dp", None), P("dp"), P("dp"), P("dp", None),
        P(), P(), P(),
    )
    return jax.shard_map(
        functools.partial(body, dims), mesh=mesh, in_specs=in_specs, out_specs=out_specs, check_vma=False
    )
```
